128 devices in a mesh: dp: 8 (over x, core), tensor: 16 (over z, y).
Axes of the slice: x: 4, y: 4, z: 4, core: 2. Of those that a mesh axis runs over, the one named last changes fastest.
Arguments:
- acts: bfloat16 [16384, 8192], P(('dp', 'tensor')), may hold values from -6 to 6
- cot_kv: bfloat16 [16384, 2048], P('dp', 'tensor'), may hold values from -0.09375 to 0.09375
- w_kv: bfloat16 [8192, 2048], P(None, 'tensor'), may hold values from -4 to 4
- feedback: bfloat16 [65536, 2048], P('dp', 'tensor'), may hold values from -3 to 3
- q_init: float32 [2048, 64], P('tensor'), may hold values from -6 to 6
Outputs:
- input_grad: bfloat16 [16384, 8192], P(('dp', 'tensor'))
- update: bfloat16 [8192, 2048], P(None, 'tensor')
- q_factor: float32 [2048, 64], P('tensor')
- new_feedback: bfloat16 [65536, 2048], P('dp', 'tensor')
The draws below stay inside these ranges and needn't reach their ends.
All inputs are finite; a program needn't handle non-finite values.
Results may differ from the reference program's by a relative error of at most 0.019.
Values may be sent and summed in bfloat16 or wider, within the bound.
No kernel may reach another device: no remote copies, remote signals or barrier semaphores. Data moves between devices by JAX's collectives and lax.ppermute only.
A program may use at most 192 MiB of HBM per device.

```python
import jax
import jax.numpy as jnp
from jax import lax

D = 8192
KVH = 8
HD = 128
RANK = 64
TOK_DEV = 128
TOK_REP = 2048
NCOL = 2048
N_DP = 8
N_TENSOR = 16


def spiked(values, key, source, target, shards_of, factor):
    owner, partner = [(jnp.arange(values.shape[position]) // (values.shape[position] // shards_of)).reshape([-1 if axis == position else 1 for axis in range(values.ndim)]) for position in (source, target)]
    chosen = jax.random.permutation(key, shards_of)[partner]
    strong = (owner == chosen) | (owner == (partner + shards_of // 2) % shards_of)
    return jnp.where(strong, factor * values, values)


def levels(stream_key, extent, shards, smallest, largest):
    level, own = 1.0, jax.random.fold_in(stream_key, 6)
    for position, parts in shards:
        draws = jnp.exp(jax.random.uniform(jax.random.fold_in(own, position), (parts,), jnp.float32, smallest / len(shards), largest / len(shards)))
        level = level * jnp.repeat(draws, extent[position] // parts).reshape([-1 if axis == position else 1 for axis in range(len(extent))])
    return level


def noise(own_key, dims, scale, reach, cuts=(), kind=jnp.bfloat16):
    array = scale * jax.random.normal(own_key, dims, jnp.float32)
    if cuts:
        array = array * levels(own_key, dims, cuts, -0.22, 0.18)
    return jnp.clip(array, -reach, reach).astype(kind)


def noise_with(key, shape, width, bound, shards, heavy, kind=jnp.bfloat16):
    entries = width * jax.random.normal(key, shape, jnp.float32)
    if shards:
        entries = entries * levels(key, shape, shards, -0.22, 0.18)
    return jnp.clip(spiked(entries, jax.random.fold_in(key, 3), *heavy), -bound, bound).astype(kind)


def setup_inputs(seed: int = 0) -> dict:
    key_of = jax.random.split(jax.random.key(seed), 6)
    return {
        "acts": noise(key_of[0], (N_DP * TOK_REP, D), 1.0, 6.0, ((0, 128),)),
        "cot_kv": noise_with(key_of[1], (N_DP * TOK_REP, NCOL), (4 * TOK_REP) ** -0.5, 0.09375, ((0, 8), (1, 16)), (1, 0, 16, 2.0)),
        "w_kv": noise(key_of[2], (D, NCOL), 0.7, 4.0, ((1, 16),)),
        "feedback": noise(key_of[3], (N_DP * D, NCOL), 0.5, 3.0, ((0, 8), (1, 16))),
        "q_init": noise(key_of[4], (NCOL, RANK), 1.0, 6.0, ((0, 16),), jnp.float32),
    }


def orthonormalize(pmat):
    gram = jnp.einsum('mdr,mds->mrs', pmat, pmat, precision=lax.Precision.HIGHEST)
    lower = jnp.linalg.cholesky(gram)
    return lax.linalg.triangular_solve(lower, pmat, left_side=False, lower=True, transpose_a=True)

def reference(acts, cot_kv, w_kv, feedback, q_init):
    tok_rep = TOK_DEV * N_TENSOR
    ncol = 2 * KVH * HD
    nmat = 2 * KVH
    qmat = q_init.reshape(nmat, HD, RANK)
    merged_all = []
    psum = jnp.zeros((nmat, D, RANK), jnp.float32)
    for rep in range(N_DP):
        rows = acts[rep * tok_rep:(rep + 1) * tok_rep].astype(jnp.float32)
        cot = cot_kv[rep * tok_rep:(rep + 1) * tok_rep].astype(jnp.float32)
        grad = jnp.dot(rows.T, cot, precision=lax.Precision.HIGHEST)
        merged = feedback[rep * D:(rep + 1) * D].astype(jnp.float32) + grad
        merged_all.append(merged)
        psum = psum + jnp.einsum('dmh,mhr->mdr', merged.reshape(D, nmat, HD), qmat, precision=lax.Precision.HIGHEST)
    phat = orthonormalize(psum / N_DP)
    qsum = jnp.zeros((nmat, HD, RANK), jnp.float32)
    for rep in range(N_DP):
        qsum = qsum + jnp.einsum('dmh,mdr->mhr', merged_all[rep].reshape(D, nmat, HD), phat, precision=lax.Precision.HIGHEST)
    qfac = qsum / N_DP
    approx = jnp.einsum('mdr,mhr->dmh', phat, qfac, precision=lax.Precision.HIGHEST).reshape(D, ncol)
    new_feedback = jnp.concatenate([(merged_all[rep] - approx).astype(jnp.bfloat16) for rep in range(N_DP)], axis=0)
    block = ncol // N_TENSOR
    cot_all = cot_kv.astype(jnp.float32)
    w_all = w_kv.astype(jnp.float32)
    total = jnp.zeros((N_DP * tok_rep, D), jnp.float32)
    for blk in range(N_TENSOR):
        part = jnp.dot(cot_all[:, blk * block:(blk + 1) * block], w_all[:, blk * block:(blk + 1) * block].T, precision=lax.Precision.HIGHEST)
        total = total + part.astype(jnp.bfloat16).astype(jnp.float32)
    input_grad = total.astype(jnp.bfloat16)
    return (input_grad, approx.astype(jnp.bfloat16), qfac.reshape(ncol, RANK), new_feedback)
```

```python
import functools

import jax
import jax.numpy as jnp
from jax import lax
from jax.experimental import pallas as pl
from jax.experimental.pallas import tpu as pltpu
from jax.sharding import PartitionSpec as P

HD = 128
RANK = 64
SIDE = 4
TILE = 512
F32 = jnp.float32
BF16 = jnp.bfloat16
HI = lax.Precision.HIGHEST


def along_tensor(array, dz, dy):
    perm = [
        (z * SIDE + y, (z + dz) % SIDE * SIDE + (y + dy) % SIDE)
        for z in range(SIDE)
        for y in range(SIDE)
    ]
    return lax.ppermute(array, "tensor", perm)


def along_dp(array, dx, dc):
    perm = [
        (x * 2 + c, (x + dx) % SIDE * 2 + (c + dc) % 2)
        for x in range(SIDE)
        for c in range(2)
    ]
    return lax.ppermute(array, "dp", perm)


def cost(flops, moved):
    return pl.CostEstimate(flops=int(flops), bytes_accessed=int(moved), transcendentals=0)


def rows_spec(rows, cols):
    return pl.BlockSpec((rows, cols), lambda j: (j, 0))


def cols_spec(rows, cols):
    return pl.BlockSpec((rows, cols), lambda j: (0, j))


def whole_spec(rows, cols):
    return pl.BlockSpec((rows, cols), lambda j: (0, 0))


def grad_kernel(a0, a1, a2lo, a2hi, a3, cmat, own, b1, b2lo, b2hi, b3):
    j = pl.program_id(0)
    mid = pl.num_programs(0) // 2
    tokens = jnp.concatenate([a0[...], a1[...], a2lo[...], a2hi[...], a3[...]], axis=0)
    part = lax.dot_general(
        tokens, cmat[...], (((0,), (0,)), ((), ())), preferred_element_type=F32
    )
    own[...] = part[:, :HD]
    b1[...] = part[:, HD : 2 * HD].astype(BF16)
    b3[...] = part[:, 3 * HD :].astype(BF16)
    across = part[:, 2 * HD : 3 * HD].astype(BF16)

    @pl.when(j < mid)
    def _():
        b2lo[...] = across

    @pl.when(j >= mid)
    def _():
        b2hi[...] = across


def grad_parts(a0, a1, a2lo, a2hi, a3, cmat):
    rows, width = a0.shape
    steps = width // TILE
    mid = steps // 2
    return pl.pallas_call(
        grad_kernel,
        grid=(steps,),
        in_specs=[
            cols_spec(rows, TILE),
            cols_spec(rows, TILE),
            cols_spec(rows // 2, TILE),
            cols_spec(rows // 2, TILE),
            cols_spec(rows, TILE),
            whole_spec(SIDE * rows, SIDE * HD),
        ],
        out_specs=[
            rows_spec(TILE, HD),
            rows_spec(TILE, HD),
            pl.BlockSpec((TILE, HD), lambda j: (jnp.minimum(j, mid - 1), 0)),
            pl.BlockSpec((TILE, HD), lambda j: (jnp.maximum(j - mid, 0), 0)),
            rows_spec(TILE, HD),
        ],
        out_shape=[
            jax.ShapeDtypeStruct((width, HD), F32),
            jax.ShapeDtypeStruct((width, HD), BF16),
            jax.ShapeDtypeStruct((width // 2, HD), BF16),
            jax.ShapeDtypeStruct((width // 2, HD), BF16),
            jax.ShapeDtypeStruct((width, HD), BF16),
        ],
        cost_estimate=cost(2 * width * SIDE * SIDE * rows * HD, 9 * width * HD * 2),
        name="grad_parts",
    )(a0, a1, a2lo, a2hi, a3, cmat)


def input_kernel(w0, wg, cmat, own, b1, b2lo, b2hi, b3):
    rows = own.shape[0]
    weights = jnp.concatenate([w0[...], wg[0, 0], wg[0, 1], wg[0, 2]], axis=1)
    part = lax.dot_general(
        cmat[...], weights, (((1,), (1,)), ((), ())), preferred_element_type=F32
    )
    own[...] = part[:rows]
    b1[...] = part[rows : 2 * rows].astype(BF16)
    b2lo[...] = part[2 * rows : 2 * rows + rows // 2].astype(BF16)
    b2hi[...] = part[2 * rows + rows // 2 : 3 * rows].astype(BF16)
    b3[...] = part[3 * rows :].astype(BF16)


def input_parts(weights, gathered, cmat, part):
    width = weights.shape[0] // 2
    rows = cmat.shape[0] // SIDE
    pieces, kinds, tile, _ = gathered.shape
    first = part * pieces
    return pl.pallas_call(
        input_kernel,
        grid=(pieces,),
        in_specs=[
            pl.BlockSpec((tile, HD), lambda j: (first + j, 0)),
            pl.BlockSpec((1, kinds // 2, tile, HD), lambda j: (j, part, 0, 0)),
            whole_spec(SIDE * rows, SIDE * HD),
        ],
        out_specs=[
            cols_spec(rows, tile),
            cols_spec(rows, tile),
            cols_spec(rows // 2, tile),
            cols_spec(rows // 2, tile),
            cols_spec(rows, tile),
        ],
        out_shape=[
            jax.ShapeDtypeStruct((rows, width), F32),
            jax.ShapeDtypeStruct((rows, width), BF16),
            jax.ShapeDtypeStruct((rows // 2, width), BF16),
            jax.ShapeDtypeStruct((rows // 2, width), BF16),
            jax.ShapeDtypeStruct((rows, width), BF16),
        ],
        cost_estimate=cost(2 * width * SIDE * SIDE * rows * HD, 9 * width * HD * 2),
        name="input_parts",
    )(weights, gathered, cmat)


def merge_kernel(fb, own, left, right, qrows, merged, keep, give):
    total = fb[...].astype(F32) + own[...] + (left[...].astype(F32) + right[...].astype(F32))
    merged[...] = total
    share = lax.dot_general(
        qrows[...], total, (((1,), (1,)), ((), ())), precision=HI, preferred_element_type=F32
    )
    keep[...] = share[: RANK // 2]
    give[...] = share[RANK // 2 :]


def merge(feedback, own, left, right, qrows, part):
    width = own.shape[0]
    tile = 1024
    steps = width // tile
    return pl.pallas_call(
        merge_kernel,
        grid=(steps,),
        in_specs=[
            pl.BlockSpec((tile, HD), lambda j: (part * steps + j, 0)),
            rows_spec(tile, HD),
            rows_spec(tile, HD),
            rows_spec(tile, HD),
            whole_spec(RANK, HD),
        ],
        out_specs=[
            rows_spec(tile, HD),
            cols_spec(RANK // 2, tile),
            cols_spec(RANK // 2, tile),
        ],
        out_shape=[
            jax.ShapeDtypeStruct((width, HD), F32),
            jax.ShapeDtypeStruct((RANK // 2, width), F32),
            jax.ShapeDtypeStruct((RANK // 2, width), F32),
        ],
        cost_estimate=cost(12 * width * RANK * HD, 14 * width * HD),
        name="merge",
    )(feedback, own, left, right, qrows)


def gram_kernel(pt, merged, gram, right):
    @pl.when(pl.program_id(0) == 0)
    def _():
        gram[...] = jnp.zeros_like(gram)
        right[...] = jnp.zeros_like(right)

    left = pt[...]
    gram[...] += lax.dot_general(
        left, left, (((1,), (1,)), ((), ())), precision=HI, preferred_element_type=F32
    )
    right[...] += jnp.dot(left, merged[...], precision=HI, preferred_element_type=F32)


def gram_of(pt, merged):
    width = merged.shape[0]
    tile = 1024
    return pl.pallas_call(
        gram_kernel,
        grid=(width // tile,),
        in_specs=[cols_spec(RANK, tile), rows_spec(tile, HD)],
        out_specs=[whole_spec(RANK, RANK), whole_spec(RANK, HD)],
        out_shape=[
            jax.ShapeDtypeStruct((RANK, RANK), F32),
            jax.ShapeDtypeStruct((RANK, HD), F32),
        ],
        cost_estimate=cost(12 * width * RANK * (RANK + HD), 6 * width * HD),
        name="gram",
    )(pt, merged)


def inverse_kernel(gram_a, gram_b, out):
    row = lax.broadcasted_iota(jnp.int32, (RANK, RANK), 0)
    col = lax.broadcasted_iota(jnp.int32, (RANK, RANK), 1)
    eye = jnp.where(row == col, 1.0, 0.0).astype(F32)
    mat = jnp.concatenate([gram_a[...] + gram_b[...], eye], axis=1)
    below = lax.broadcasted_iota(jnp.int32, (RANK, 1), 0)
    for k in range(RANK - 1):
        pivot = mat[k : k + 1, :]
        column = mat[:, k : k + 1]
        factor = jnp.where(below > k, column / mat[k : k + 1, k : k + 1], 0.0)
        mat = mat - factor * pivot
    diag = jnp.sum(jnp.where(row == col, mat[:, :RANK], 0.0), axis=1, keepdims=True)
    out[...] = mat[:, RANK:] / jnp.sqrt(diag)


def inverse_factor(gram_a, gram_b):
    return pl.pallas_call(
        inverse_kernel,
        out_shape=jax.ShapeDtypeStruct((RANK, RANK), F32),
        cost_estimate=cost(RANK * RANK * RANK * 400, RANK * RANK * 16),
        name="inverse_factor",
    )(gram_a, gram_b)


def final_kernel(inv, rsum, pt_a, pt_b, mg_a, mg_b, qt, update, newfb, zmat):
    j = pl.program_id(0)
    mid = pl.num_programs(0) // 2

    @pl.when(j == 0)
    def _():
        right = jnp.dot(inv[...], rsum[...], precision=HI, preferred_element_type=F32) * 0.125
        qt[...] = right
        zmat[...] = lax.dot_general(
            inv[...], right, (((0,), (0,)), ((), ())), precision=HI, preferred_element_type=F32
        )

    def finish(pt, mg):
        approx = lax.dot_general(
            pt[...], zmat[...], (((0,), (0,)), ((), ())), precision=HI, preferred_element_type=F32
        )
        update[...] = approx.astype(BF16)
        newfb[...] = (mg[...] - approx).astype(BF16)

    @pl.when(j < mid)
    def _():
        finish(pt_a, mg_a)

    @pl.when(j >= mid)
    def _():
        finish(pt_b, mg_b)


def final(inv, rsum, pts, mgs):
    half = mgs[0].shape[0]
    tile = 1024
    mid = half // tile
    lo = lambda j: jnp.minimum(j, mid - 1)
    hi = lambda j: jnp.maximum(j - mid, 0)
    return pl.pallas_call(
        final_kernel,
        grid=(2 * mid,),
        in_specs=[
            whole_spec(RANK, RANK),
            whole_spec(RANK, HD),
            pl.BlockSpec((RANK, tile), lambda j: (0, lo(j))),
            pl.BlockSpec((RANK, tile), lambda j: (0, hi(j))),
            pl.BlockSpec((tile, HD), lambda j: (lo(j), 0)),
            pl.BlockSpec((tile, HD), lambda j: (hi(j), 0)),
        ],
        out_specs=[
            whole_spec(RANK, HD),
            rows_spec(tile, HD),
            rows_spec(tile, HD),
        ],
        out_shape=[
            jax.ShapeDtypeStruct((RANK, HD), F32),
            jax.ShapeDtypeStruct((2 * half, HD), BF16),
            jax.ShapeDtypeStruct((2 * half, HD), BF16),
        ],
        scratch_shapes=[pltpu.VMEM((RANK, HD), F32)],
        cost_estimate=cost(24 * half * RANK * HD, 24 * half * HD),
        name="final",
    )(inv, rsum, *pts, *mgs)


def gather_line(block, step):
    rows = block.shape[0]
    before = step(block, 1)
    after = step(block, -1)
    across_lo = step(before[: rows // 2], 1)
    across_hi = step(after[rows // 2 :], -1)
    return block, after, across_lo, across_hi, before


def scatter_line(b1, b2lo, b2hi, b3, step):
    rows = b1.shape[0]
    low = step(b2lo, 1)
    high = step(b2hi, -1)
    up = jnp.concatenate(
        [(b1[: rows // 2].astype(F32) + low.astype(F32)).astype(BF16), b1[rows // 2 :]], axis=0
    )
    down = jnp.concatenate(
        [b3[: rows // 2], (b3[rows // 2 :].astype(F32) + high.astype(F32)).astype(BF16)], axis=0
    )
    return step(up, 1), step(down, -1)


def sum_chips(array):
    ahead = along_dp(array, 1, 0).astype(F32)
    behind = along_dp(array, -1, 0).astype(F32)
    across = along_dp(array, 2, 0).astype(F32)
    return (array.astype(F32) + across) + (ahead + behind)


def sum_left(keep, give, core):
    chip = (keep + along_dp(give, 0, 1)).astype(BF16)
    mine = sum_chips(chip)
    theirs = along_dp(mine, 0, 1)
    first = jnp.where(core == 0, mine, theirs)
    second = jnp.where(core == 0, theirs, mine)
    return jnp.concatenate([first, second], axis=0)


def sum_right(part):
    return sum_chips(part + along_dp(part, 0, 1))


def local(acts, cot_kv, w_kv, feedback, q_init):
    tokens, width = acts.shape
    half = width // 2
    replicas = lax.axis_size("dp")
    place = lax.axis_index("dp")
    core = place % 2
    spot = lax.axis_index("tensor")
    z, y = spot // SIDE, spot % SIDE
    in_y = lambda array, k: along_tensor(array, 0, k)
    in_z = lambda array, k: along_tensor(array, k, 0)

    parts = (
        gather_line(acts[:, :half], in_y),
        gather_line(acts[:, half:], in_z),
    )

    blocks = cot_kv.reshape(SIDE, SIDE, tokens, HD)
    blocks = jnp.concatenate([blocks, blocks], axis=1)
    blocks = jnp.concatenate([blocks, blocks], axis=0)
    blocks = lax.dynamic_slice(blocks, (z, y, 0, 0), (SIDE, SIDE, tokens, HD))
    piece = half // replicas
    w_lo = lax.dynamic_slice(w_kv, (place * piece, 0), (piece, HD))
    w_hi = lax.dynamic_slice(w_kv, (half + place * piece, 0), (piece, HD))
    flat = SIDE * tokens
    cols = {0: blocks[0].reshape(flat, HD)}
    rows = {0: blocks[:, 0].reshape(flat, HD)}
    w_parts = {}
    for k in range(1, SIDE):
        got = in_z(jnp.concatenate([blocks[k].reshape(flat, HD), w_lo], axis=0), k)
        cols[SIDE - k], w_parts[SIDE - k - 1] = got[:flat], got[flat:]
        got = in_y(jnp.concatenate([blocks[:, k].reshape(flat, HD), w_hi], axis=0), k)
        rows[SIDE - k], w_parts[2 * SIDE - k - 2] = got[:flat], got[flat:]
    cmat = (
        jnp.concatenate([cols[k] for k in range(SIDE)], axis=1),
        jnp.concatenate([rows[k] for k in range(SIDE)], axis=1),
    )
    gathered = lax.all_gather(
        jnp.stack([w_parts[k] for k in range(2 * SIDE - 2)]), "dp", axis=0
    )

    qcols = q_init.T
    qrows = jnp.where(
        core == 0, qcols, jnp.concatenate([qcols[RANK // 2 :], qcols[: RANK // 2]], axis=0)
    )

    mgs, pts, grams, rights = [], [], [], []
    for part, step in ((0, in_z), (1, in_y)):
        own, b1, b2lo, b2hi, b3 = grad_parts(*parts[part], cmat[part])
        left, right = scatter_line(b1, b2lo, b2hi, b3, step)
        merged, keep, give = merge(feedback, own, left, right, qrows, part)
        pt = sum_left(keep, give, core)
        gram, share = gram_of(pt, merged)
        mgs.append(merged)
        pts.append(pt)
        grams.append(gram)
        rights.append(share)

    ig = []
    for part, step in ((0, in_y), (1, in_z)):
        own, b1, b2lo, b2hi, b3 = input_parts(w_kv, gathered, cmat[part], part)
        left, right = scatter_line(b1, b2lo, b2hi, b3, step)
        ig.append((own + (left.astype(F32) + right.astype(F32))).astype(BF16))
    input_grad = jnp.concatenate(ig, axis=1)

    inv = inverse_factor(*grams)
    rsum = sum_right(rights[0] + rights[1])
    qt, update, new_feedback = final(inv, rsum, pts, mgs)
    return input_grad, update, qt.T, new_feedback


def solution(mesh):
    placed = (
        P(("dp", "tensor"), None),
        P("dp", "tensor"),
        P(None, "tensor"),
        P("dp", "tensor"),
        P("tensor", None),
    )
    return jax.shard_map(
        local,
        mesh=mesh,
        in_specs=placed,
        out_specs=(
            P(("dp", "tensor"), None),
            P(None, "tensor"),
            P("tensor", None),
            P("dp", "tensor"),
        ),
        check_vma=False,
    )
```

```python
import jax
import jax.numpy as jnp
from jax import lax
from jax.experimental import pallas as pl
from jax.experimental.pallas import tpu as pltpu
from jax.sharding import PartitionSpec as P

HD = 128
RANK = 64
SIDE = 4
TILE = 2048
WIDE = 2048
PART = 1024
F32 = jnp.float32
BF16 = jnp.bfloat16
HI = lax.Precision.HIGHEST
NN = (((1,), (0,)), ((), ()))
NT = (((1,), (1,)), ((), ()))
TN = (((0,), (0,)), ((), ()))


def along_tensor(array, dz, dy):
    perm = [
        (z * SIDE + y, (z + dz) % SIDE * SIDE + (y + dy) % SIDE)
        for z in range(SIDE)
        for y in range(SIDE)
    ]
    return lax.ppermute(array, "tensor", perm)


def along_dp(array, target):
    perm = []
    for x in range(SIDE):
        for c in range(2):
            to_x, to_c = target(x, c)
            perm.append((x * 2 + c, to_x % SIDE * 2 + to_c))
    return lax.ppermute(array, "dp", perm)


def other_core(array):
    return along_dp(array, lambda x, c: (x, 1 - c))


def cost(flops, moved):
    return pl.CostEstimate(flops=int(flops), bytes_accessed=int(moved), transcendentals=0)


def cols_spec(rows, cols):
    return pl.BlockSpec((rows, cols), lambda j: (0, j))


def rows_spec(rows, cols):
    return pl.BlockSpec((rows, cols), lambda j: (j, 0))


def whole_spec(rows, cols):
    return pl.BlockSpec((rows, cols), lambda j: (0, 0))


ANY_SPEC = pl.BlockSpec(memory_space=pl.ANY)
SMEM_SPEC = pl.BlockSpec(memory_space=pltpu.SMEM)


def halves(array):
    high = array.astype(BF16)
    return high, (array - high.astype(F32)).astype(BF16)


def dot3(left, right, dims):
    dot = lambda a, b: lax.dot_general(a, b, dims, preferred_element_type=F32)
    return dot(left[0], right[0]) + (dot(left[0], right[1]) + dot(left[1], right[0]))


def grad_kernel(spots, a0, a1, a2lo, a2hi, a3, cots, own, up, down, rest, cturn):
    j = pl.program_id(0)
    mid = pl.num_programs(0) // 2

    @pl.when(j == 0)
    def _():
        for r in range(SIDE):
            block = cots.at[(spots[0] + r) % SIDE]
            for s in range(SIDE):
                rows = pl.ds(pl.multiple_of((spots[1] + s) % SIDE * HD, HD), HD)
                cturn[r * HD : (r + 1) * HD, s * HD : (s + 1) * HD] = block[rows, :].T

    tokens = jnp.concatenate([a0[...], a1[...], a2lo[...], a2hi[...], a3[...]], axis=0)
    grads = lax.dot_general(cturn[...], tokens, NN, preferred_element_type=F32)
    own[...] = grads[:HD]
    ahead = grads[HD : 2 * HD].astype(BF16)
    across = grads[2 * HD : 3 * HD].astype(BF16)
    behind = grads[3 * HD :].astype(BF16)

    @pl.when(j < mid)
    def _():
        up[...] = across
        down[...] = behind
        rest[...] = ahead

    @pl.when(j >= mid)
    def _():
        up[...] = ahead
        down[...] = across
        rest[...] = behind


def grad_parts(spots, pieces, cots):
    rows, width = pieces[0].shape
    flat = SIDE * rows
    mid = width // TILE // 2
    stacked = pl.BlockSpec((HD, TILE), lambda j: (j // mid, j % mid))
    return pl.pallas_call(
        grad_kernel,
        grid=(width // TILE,),
        in_specs=[SMEM_SPEC]
        + [cols_spec(piece.shape[0], TILE) for piece in pieces]
        + [pl.BlockSpec((SIDE, flat, HD), lambda j: (0, 0, 0))],
        out_specs=[cols_spec(HD, TILE)] + [stacked] * 3,
        out_shape=[jax.ShapeDtypeStruct((HD, width), F32)]
        + [jax.ShapeDtypeStruct((2 * HD, width // 2), BF16)] * 3,
        scratch_shapes=[pltpu.VMEM((SIDE * HD, flat), BF16)],
        cost_estimate=cost(2 * width * SIDE * flat * HD, 9 * width * HD * 2),
        name="grad_parts",
    )(spots, *pieces, cots)


def input_product(mine, theirs, cots):
    first = pl.program_id(0) < pl.num_programs(0) // 2
    weights = jnp.concatenate(
        [jnp.where(first, mine[k], theirs[k]) for k in range(SIDE)], axis=1
    )
    return lax.dot_general(cots, weights, NT, preferred_element_type=F32)


def input_kernel(spots, mine, theirs, cots, out):
    lined = jnp.concatenate([cots[k] for k in range(SIDE)], axis=1)
    out[...] = input_product(mine, theirs, lined).astype(BF16)


def input_parts(spots, gathered, cots):
    piece = gathered[0].shape[1]
    flat = cots.shape[1]
    mid = piece // PART
    place = lambda j, spots: (spots[2] + j // mid) % 2 * mid + j % mid
    return pl.pallas_call(
        input_kernel,
        grid_spec=pltpu.PrefetchScalarGridSpec(
            num_scalar_prefetch=1,
            grid=(2 * mid,),
            in_specs=[
                pl.BlockSpec((SIDE, PART, HD), lambda j, spots: (0, jnp.minimum(j, mid - 1), 0)),
                pl.BlockSpec((SIDE, PART, HD), lambda j, spots: (0, jnp.maximum(j - mid, 0), 0)),
                pl.BlockSpec((SIDE, flat, HD), lambda j, spots: (0, 0, 0)),
            ],
            out_specs=pl.BlockSpec((flat, PART), lambda j, spots: (0, place(j, spots))),
        ),
        out_shape=jax.ShapeDtypeStruct((flat, 2 * piece), BF16),
        cost_estimate=cost(4 * piece * SIDE * flat * HD, 18 * piece * HD * 2),
        name="input_parts",
    )(spots, *gathered, cots)


def merge_kernel(fb, own, pl_lo, pl_hi, su_lo, su_hi, qrows, *refs):
    merged, keep, give = refs[-3:]
    j = pl.program_id(0)
    mid = pl.num_programs(0) // 2
    base = fb[...].astype(F32) + own[...]

    def finish(plain, summed):
        total = base + (plain[...].astype(F32) + summed[...].astype(F32))
        merged[...] = total
        share = dot3(halves(qrows[...]), halves(total), NN)
        keep[...] = share[: RANK // 2]
        give[...] = share[RANK // 2 :]

    @pl.when(j < mid)
    def _():
        finish(pl_lo, su_lo)

    @pl.when(j >= mid)
    def _():
        finish(pl_hi, su_hi)


def merge(feedback, own, sums, qrows, part, before):
    got_up, got_down, sum_up, sum_down = sums
    width = own.shape[1]
    steps = width // WIDE
    mid = steps // 2
    first = part * steps
    shifted = lambda rows: pl.BlockSpec((rows, WIDE), lambda j: (0, first + j))
    low = pl.BlockSpec((HD, WIDE), lambda j: (0, jnp.minimum(j, mid - 1)))
    high = pl.BlockSpec((HD, WIDE), lambda j: (1, jnp.maximum(j - mid, 0)))
    high_from = pl.BlockSpec((HD, WIDE), lambda j: (0, jnp.maximum(j - mid, 0)))
    return pl.pallas_call(
        merge_kernel,
        grid=(steps,),
        in_specs=[shifted(HD), cols_spec(HD, WIDE), low, high, low, high_from, whole_spec(RANK, HD)]
        + [ANY_SPEC] * len(before),
        out_specs=[shifted(HD), shifted(RANK // 2), shifted(RANK // 2)],
        out_shape=[
            jax.ShapeDtypeStruct((HD, 2 * width), F32),
            jax.ShapeDtypeStruct((RANK // 2, 2 * width), F32),
            jax.ShapeDtypeStruct((RANK // 2, 2 * width), F32),
        ],
        input_output_aliases={7 + k: k for k in range(len(before))},
        cost_estimate=cost(6 * width * RANK * HD, 14 * width * HD),
        name="merge",
    )(feedback, own, got_down, got_up, sum_up, sum_down, qrows, *before)


def ordered(core, mine, theirs):
    first = jnp.where(core == 0, mine[...], theirs[...])
    second = jnp.where(core == 0, theirs[...], mine[...])
    return jnp.concatenate([first, second], axis=0)


def gram_kernel(spots, mine, theirs, merged, right, gram):
    @pl.when(pl.program_id(0) == 0)
    def _():
        gram[...] = jnp.zeros_like(gram)
        right[...] = jnp.zeros_like(right)

    pt = halves(ordered(spots[2], mine, theirs))
    right[...] += dot3(halves(merged[...]), pt, NT)
    gram[...] += dot3(pt, pt, NT)


def gram_of(spots, mine, theirs, merged):
    width = merged.shape[1]
    half = RANK // 2
    return pl.pallas_call(
        gram_kernel,
        grid=(width // WIDE,),
        in_specs=[SMEM_SPEC, cols_spec(half, WIDE), cols_spec(half, WIDE), cols_spec(HD, WIDE)],
        out_specs=[whole_spec(HD, RANK), whole_spec(RANK, RANK)],
        out_shape=[
            jax.ShapeDtypeStruct((HD, RANK), F32),
            jax.ShapeDtypeStruct((RANK, RANK), F32),
        ],
        cost_estimate=cost(6 * width * RANK * (RANK + HD), 6 * width * HD),
        name="gram",
    )(spots, mine, theirs, merged)


def inverse_kernel(gram, out):
    row = lax.broadcasted_iota(jnp.int32, (RANK, RANK), 0)
    col = lax.broadcasted_iota(jnp.int32, (RANK, RANK), 1)
    eye = jnp.where(row == col, 1.0, 0.0).astype(F32)
    mat = jnp.concatenate([gram[...], eye], axis=1)
    below = lax.broadcasted_iota(jnp.int32, (RANK, 1), 0)
    for k in range(RANK - 1):
        pivot = mat[k : k + 1, :]
        column = mat[:, k : k + 1]
        factor = jnp.where(below > k, column / mat[k : k + 1, k : k + 1], 0.0)
        mat = mat - factor * pivot
    diag = jnp.sum(jnp.where(row == col, mat[:, :RANK], 0.0), axis=1, keepdims=True)
    out[...] = mat[:, RANK:] / jnp.sqrt(diag)


def inverse_factor(gram):
    return pl.pallas_call(
        inverse_kernel,
        out_shape=jax.ShapeDtypeStruct((RANK, RANK), F32),
        cost_estimate=cost(RANK * RANK * RANK * 400, RANK * RANK * 16),
        name="inverse_factor",
    )(gram)


def final_kernel(replicas, spots, inv, rsum, mine, theirs, merged, qt, update, newfb, zhi, zlo):
    @pl.when(pl.program_id(0) == 0)
    def _():
        right = lax.dot_general(inv[...], rsum[...], NT, precision=HI, preferred_element_type=F32)
        right = right * (1.0 / replicas)
        qt[...] = right
        zturn = lax.dot_general(right, inv[...], TN, precision=HI, preferred_element_type=F32)
        zhi[...], zlo[...] = halves(zturn)

    pt = halves(ordered(spots[2], mine, theirs))
    approx = dot3((zhi[...], zlo[...]), pt, NN)
    update[...] = approx.astype(BF16).T
    newfb[...] = (merged[...] - approx).astype(BF16).T


def final(spots, inv, rsum, mine, theirs, merged, replicas):
    width = merged.shape[1]
    half = RANK // 2
    return pl.pallas_call(
        lambda *refs: final_kernel(replicas, *refs),
        grid=(width // WIDE,),
        in_specs=[
            SMEM_SPEC,
            whole_spec(RANK, RANK),
            whole_spec(HD, RANK),
            cols_spec(half, WIDE),
            cols_spec(half, WIDE),
            cols_spec(HD, WIDE),
        ],
        out_specs=[whole_spec(RANK, HD), rows_spec(WIDE, HD), rows_spec(WIDE, HD)],
        out_shape=[
            jax.ShapeDtypeStruct((RANK, HD), F32),
            jax.ShapeDtypeStruct((width, HD), BF16),
            jax.ShapeDtypeStruct((width, HD), BF16),
        ],
        scratch_shapes=[pltpu.VMEM((HD, RANK), BF16)] * 2,
        cost_estimate=cost(6 * width * RANK * HD, 12 * width * HD),
        name="final",
    )(spots, inv, rsum, mine, theirs, merged)


def tied(arrays, others):
    return lax.optimization_barrier((arrays, others))[0]


def neighbours(block, step):
    return step(block, 1), step(block, -1)


def to_pass_on(before, after):
    rows = before.shape[0]
    return before[: rows // 2], after[rows // 2 :]


def gather_line(block, before, after, passed, step):
    return block, after, step(passed[0], 1), step(passed[1], -1), before


def scatter_near(up, down, step):
    return step(up, 1), step(down, -1)


def scatter_far(got_up, got_down, rest, step):
    mid = rest.shape[0] // 2
    low = lambda array: array[:mid].astype(F32)
    high = lambda array: array[mid:].astype(F32)
    sum_up = step((low(rest) + low(got_up)).astype(BF16), 1)
    sum_down = step((high(rest) + high(got_down)).astype(BF16), -1)
    return got_up, got_down, sum_up, sum_down


def sum_left(keep, give):
    chip = (keep + other_core(give)).astype(BF16)
    mid = chip.shape[0] // 2
    near = lambda array: along_dp(array, lambda x, c: (x ^ 1, c))
    far = lambda array: along_dp(array, lambda x, c: (3 - x, c))
    add = lambda a, b: a.astype(F32) + b.astype(F32)
    first, second = chip[:mid], chip[mid:]
    first_pair = add(first, near(first)).astype(BF16)
    second_pair = add(second, far(second)).astype(BF16)
    mine = jnp.concatenate(
        [add(first_pair, far(first_pair)), add(second_pair, near(second_pair))], axis=0
    )
    return mine, other_core(mine)


def sum_right(part):
    chip = part + other_core(part)
    ahead = along_dp(chip, lambda x, c: (x + 1, c))
    behind = along_dp(chip, lambda x, c: (x - 1, c))
    across = along_dp(chip, lambda x, c: (x + 2, c))
    return (chip + across) + (ahead + behind)


def local(acts, cot_kv, w_kv, feedback, q_init):
    tokens, width = acts.shape
    half = width // 2
    replicas = lax.axis_size("dp")
    place = lax.axis_index("dp")
    core = place % 2
    spot = lax.axis_index("tensor")
    z, y = spot // SIDE, spot % SIDE
    spots = jnp.stack([z, y, core]).astype(jnp.int32)
    in_y = lambda array, k: along_tensor(array, 0, k)
    in_z = lambda array, k: along_tensor(array, k, 0)
    lines_z = [[z * SIDE + y for z in range(SIDE)] for y in range(SIDE)]
    lines_y = [[z * SIDE + y for y in range(SIDE)] for z in range(SIDE)]
    flat = SIDE * tokens

    blocks = acts[:, :half], acts[:, half:]
    near = neighbours(blocks[0], in_y)
    cots = lax.all_to_all(
        cot_kv, "tensor", 0, 0, axis_index_groups=lines_z, tiled=True
    ).reshape(SIDE, flat, HD)
    share = lax.dynamic_slice(w_kv, (core * half, 0), (half, HD))
    weights = lax.all_gather(share, "tensor", axis=0, axis_index_groups=lines_z)

    fb_turned = feedback.T
    qcols = q_init.T
    qrows = jnp.where(
        core == 0, qcols, jnp.concatenate([qcols[RANK // 2 :], qcols[: RANK // 2]], axis=0)
    )
    near, fb_turned, qrows, cots = lax.optimization_barrier((near, fb_turned, qrows, cots))
    pieces = gather_line(blocks[0], *near, to_pass_on(*near), in_y)
    near = neighbours(tied(blocks[1], pieces), in_y)
    own_a, up, down, rest_a = grad_parts(spots, pieces, cots)
    got_a = scatter_near(up, down, in_z)
    near, up = lax.optimization_barrier((near, up))
    passed = tied(to_pass_on(*near), got_a)
    pieces = gather_line(blocks[1], *near, passed, in_y)

    weights = tied(weights, (near, got_a))
    shares = input_parts(spots, (weights, other_core(weights)), cots)
    sums_a = scatter_far(*got_a, rest_a, in_z)

    pieces, sums_a, shares = lax.optimization_barrier((pieces, sums_a, shares))
    own_b, up, down, rest_b = grad_parts(spots, pieces, cots)
    got_b = scatter_near(up, down, in_z)
    input_grad = lax.psum_scatter(
        tied(shares, up), "tensor", scatter_dimension=0, axis_index_groups=lines_y, tiled=True
    )

    left = merge(fb_turned, own_a, tied(sums_a, got_b), qrows, 0, ())
    sums_b = scatter_far(*got_b, rest_b, in_z)
    sums_b, left = lax.optimization_barrier((sums_b, left))
    merged, keep, give = merge(fb_turned, own_b, sums_b, qrows, 1, left)
    mine, theirs = sum_left(keep, give)
    right, gram = gram_of(spots, mine, theirs, merged)
    inv = inverse_factor(gram)
    rsum = sum_right(right)
    qt, update, new_feedback = final(spots, inv, rsum, mine, theirs, merged, replicas)
    return input_grad, update, qt.T, new_feedback


def solution(mesh):
    placed = (
        P(("dp", "tensor"), None),
        P("dp", "tensor"),
        P(None, "tensor"),
        P("dp", "tensor"),
        P("tensor", None),
    )
    return jax.shard_map(
        local,
        mesh=mesh,
        in_specs=placed,
        out_specs=(
            P(("dp", "tensor"), None),
            P(None, "tensor"),
            P("tensor", None),
            P("dp", "tensor"),
        ),
        check_vma=False,
    )
```

```python
import jax
import jax.numpy as jnp
from jax import lax
from jax.experimental import pallas as pl
from jax.experimental.pallas import tpu as pltpu
from jax.sharding import PartitionSpec as P

HD = 128
RANK = 64
SIDE = 4
TILE = 2048
WIDE = 2048
LONG = 4096
VMEM = 40 * 1024 * 1024
PART = 1024
F32 = jnp.float32
BF16 = jnp.bfloat16
HI = lax.Precision.HIGHEST
NN = (((1,), (0,)), ((), ()))
NT = (((1,), (1,)), ((), ()))
TN = (((0,), (0,)), ((), ()))


def along_tensor(array, dz, dy):
    perm = [
        (z * SIDE + y, (z + dz) % SIDE * SIDE + (y + dy) % SIDE)
        for z in range(SIDE)
        for y in range(SIDE)
    ]
    return lax.ppermute(array, "tensor", perm)


def along_dp(array, target):
    perm = []
    for x in range(SIDE):
        for c in range(2):
            to_x, to_c = target(x, c)
            perm.append((x * 2 + c, to_x % SIDE * 2 + to_c))
    return lax.ppermute(array, "dp", perm)


def other_core(array):
    return along_dp(array, lambda x, c: (x, 1 - c))


def cost(flops, moved):
    return pl.CostEstimate(flops=int(flops), bytes_accessed=int(moved), transcendentals=0)


def cols_spec(rows, cols):
    return pl.BlockSpec((rows, cols), lambda j: (0, j))


def rows_spec(rows, cols):
    return pl.BlockSpec((rows, cols), lambda j: (j, 0))


def whole_spec(rows, cols):
    return pl.BlockSpec((rows, cols), lambda j: (0, 0))


ANY_SPEC = pl.BlockSpec(memory_space=pl.ANY)
SMEM_SPEC = pl.BlockSpec(memory_space=pltpu.SMEM)


def halves(array):
    high = array.astype(BF16)
    return high, (array - high.astype(F32)).astype(BF16)


def dot3(left, right, dims):
    dot = lambda a, b: lax.dot_general(a, b, dims, preferred_element_type=F32)
    return dot(left[0], right[0]) + (dot(left[0], right[1]) + dot(left[1], right[0]))


def turn_kernel(spots, cots, cturn):
    for r in range(SIDE):
        block = cots.at[(spots[0] + r) % SIDE]
        for s in range(SIDE):
            rows = pl.ds(pl.multiple_of((spots[1] + s) % SIDE * HD, HD), HD)
            cturn[r * HD : (r + 1) * HD, s * HD : (s + 1) * HD] = block[rows, :].T


def turn_cots(spots, cots):
    flat = cots.shape[1]
    return pl.pallas_call(
        turn_kernel,
        in_specs=[SMEM_SPEC, pl.BlockSpec(memory_space=pltpu.VMEM)],
        out_specs=pl.BlockSpec(memory_space=pltpu.VMEM),
        out_shape=jax.ShapeDtypeStruct((SIDE * HD, flat), BF16),
        cost_estimate=cost(0, 4 * SIDE * HD * flat),
        name="turn_cots",
    )(spots, cots)


def grad_kernel(a0, a1, a2lo, a2hi, a3, cturn, own, up, down, rest):
    j = pl.program_id(0)
    mid = pl.num_programs(0) // 2
    tokens = jnp.concatenate([a0[...], a1[...], a2lo[...], a2hi[...], a3[...]], axis=0)
    grads = lax.dot_general(cturn[...], tokens, NN, preferred_element_type=F32)
    own[...] = grads[:HD]
    ahead = grads[HD : 2 * HD].astype(BF16)
    across = grads[2 * HD : 3 * HD].astype(BF16)
    behind = grads[3 * HD :].astype(BF16)

    @pl.when(j < mid)
    def _():
        up[...] = across
        down[...] = behind
        rest[...] = ahead

    @pl.when(j >= mid)
    def _():
        up[...] = ahead
        down[...] = across
        rest[...] = behind


def grad_parts(pieces, cturn):
    rows, width = pieces[0].shape
    flat = SIDE * rows
    mid = width // TILE // 2
    stacked = pl.BlockSpec((HD, TILE), lambda j: (j // mid, j % mid))
    return pl.pallas_call(
        grad_kernel,
        grid=(width // TILE,),
        in_specs=[cols_spec(piece.shape[0], TILE) for piece in pieces]
        + [whole_spec(SIDE * HD, flat)],
        out_specs=[cols_spec(HD, TILE)] + [stacked] * 3,
        out_shape=[jax.ShapeDtypeStruct((HD, width), F32)]
        + [jax.ShapeDtypeStruct((2 * HD, width // 2), BF16)] * 3,
        cost_estimate=cost(2 * width * SIDE * flat * HD, 9 * width * HD * 2),
        name="grad_parts",
    )(*pieces, cturn)


def input_product(mine, theirs, cots):
    first = pl.program_id(0) < pl.num_programs(0) // 2
    weights = jnp.concatenate(
        [jnp.where(first, mine[k], theirs[k]) for k in range(SIDE)], axis=1
    )
    return lax.dot_general(cots, weights, NT, preferred_element_type=F32)


def input_kernel(spots, mine, theirs, cots, out):
    lined = jnp.concatenate([cots[k] for k in range(SIDE)], axis=1)
    out[...] = input_product(mine, theirs, lined).astype(BF16)


def input_parts(spots, gathered, cots):
    piece = gathered[0].shape[1]
    flat = cots.shape[1]
    mid = piece // PART
    place = lambda j, spots: (spots[2] + j // mid) % 2 * mid + j % mid
    return pl.pallas_call(
        input_kernel,
        grid_spec=pltpu.PrefetchScalarGridSpec(
            num_scalar_prefetch=1,
            grid=(2 * mid,),
            in_specs=[
                pl.BlockSpec((SIDE, PART, HD), lambda j, spots: (0, jnp.minimum(j, mid - 1), 0)),
                pl.BlockSpec((SIDE, PART, HD), lambda j, spots: (0, jnp.maximum(j - mid, 0), 0)),
                pl.BlockSpec((SIDE, flat, HD), lambda j, spots: (0, 0, 0)),
            ],
            out_specs=pl.BlockSpec((flat, PART), lambda j, spots: (0, place(j, spots))),
        ),
        out_shape=jax.ShapeDtypeStruct((flat, 2 * piece), BF16),
        cost_estimate=cost(4 * piece * SIDE * flat * HD, 18 * piece * HD * 2),
        name="input_parts",
    )(spots, *gathered, cots)


def merge_kernel(fb, own, pl_lo, pl_hi, su_lo, su_hi, qrows, *refs):
    merged, keep, give = refs[-3:]
    j = pl.program_id(0)
    mid = pl.num_programs(0) // 2
    base = fb[...].astype(F32) + own[...]

    def finish(plain, summed):
        total = base + (plain[...].astype(F32) + summed[...].astype(F32))
        merged[...] = total
        share = dot3(halves(qrows[...]), halves(total), NN)
        keep[...] = share[: RANK // 2]
        give[...] = share[RANK // 2 :]

    @pl.when(j < mid)
    def _():
        finish(pl_lo, su_lo)

    @pl.when(j >= mid)
    def _():
        finish(pl_hi, su_hi)


def merge(feedback, own, sums, qrows, part, before):
    got_up, got_down, sum_up, sum_down = sums
    width = own.shape[1]
    steps = width // WIDE
    mid = steps // 2
    first = part * steps
    shifted = lambda rows: pl.BlockSpec((rows, WIDE), lambda j: (0, first + j))
    low = pl.BlockSpec((HD, WIDE), lambda j: (0, jnp.minimum(j, mid - 1)))
    high = pl.BlockSpec((HD, WIDE), lambda j: (1, jnp.maximum(j - mid, 0)))
    high_from = pl.BlockSpec((HD, WIDE), lambda j: (0, jnp.maximum(j - mid, 0)))
    return pl.pallas_call(
        merge_kernel,
        grid=(steps,),
        in_specs=[shifted(HD), cols_spec(HD, WIDE), low, high, low, high_from, whole_spec(RANK, HD)]
        + [ANY_SPEC] * len(before),
        out_specs=[shifted(HD), shifted(RANK // 2), shifted(RANK // 2)],
        out_shape=[
            jax.ShapeDtypeStruct((HD, 2 * width), F32),
            jax.ShapeDtypeStruct((RANK // 2, 2 * width), F32),
            jax.ShapeDtypeStruct((RANK // 2, 2 * width), F32),
        ],
        input_output_aliases={7 + k: k for k in range(len(before))},
        cost_estimate=cost(6 * width * RANK * HD, 14 * width * HD),
        name="merge",
    )(feedback, own, got_down, got_up, sum_up, sum_down, qrows, *before)


def ordered(core, mine, theirs):
    first = jnp.where(core == 0, mine[...], theirs[...])
    second = jnp.where(core == 0, theirs[...], mine[...])
    return jnp.concatenate([first, second], axis=0)


def gram_kernel(spots, mine, theirs, merged, right, gram):
    @pl.when(pl.program_id(0) == 0)
    def _():
        gram[...] = jnp.zeros_like(gram)
        right[...] = jnp.zeros_like(right)

    pt = halves(ordered(spots[2], mine, theirs))
    right[...] += dot3(halves(merged[...]), pt, NT)
    gram[...] += dot3(pt, pt, NT)


def gram_of(spots, mine, theirs, merged):
    width = merged.shape[1]
    half = RANK // 2
    return pl.pallas_call(
        gram_kernel,
        grid=(width // LONG,),
        in_specs=[SMEM_SPEC, cols_spec(half, LONG), cols_spec(half, LONG), cols_spec(HD, LONG)],
        out_specs=[whole_spec(HD, RANK), whole_spec(RANK, RANK)],
        out_shape=[
            jax.ShapeDtypeStruct((HD, RANK), F32),
            jax.ShapeDtypeStruct((RANK, RANK), F32),
        ],
        cost_estimate=cost(6 * width * RANK * (RANK + HD), 6 * width * HD),
        compiler_params=pltpu.CompilerParams(vmem_limit_bytes=VMEM),
        name="gram",
    )(spots, mine, theirs, merged)


def inverse_kernel(gram, out):
    row = lax.broadcasted_iota(jnp.int32, (RANK, RANK), 0)
    col = lax.broadcasted_iota(jnp.int32, (RANK, RANK), 1)
    eye = jnp.where(row == col, 1.0, 0.0).astype(F32)
    mat = jnp.concatenate([gram[...], eye], axis=1)
    below = lax.broadcasted_iota(jnp.int32, (RANK, 1), 0)
    for k in range(RANK - 1):
        pivot = mat[k : k + 1, :]
        column = mat[:, k : k + 1]
        factor = jnp.where(below > k, column / mat[k : k + 1, k : k + 1], 0.0)
        mat = mat - factor * pivot
    diag = jnp.sum(jnp.where(row == col, mat[:, :RANK], 0.0), axis=1, keepdims=True)
    out[...] = mat[:, RANK:] / jnp.sqrt(diag)


def inverse_factor(gram):
    return pl.pallas_call(
        inverse_kernel,
        out_shape=jax.ShapeDtypeStruct((RANK, RANK), F32),
        cost_estimate=cost(RANK * RANK * RANK * 400, RANK * RANK * 16),
        name="inverse_factor",
    )(gram)


def final_kernel(replicas, spots, inv, rsum, mine, theirs, merged, qt, update, newfb, zhi, zlo):
    @pl.when(pl.program_id(0) == 0)
    def _():
        right = lax.dot_general(inv[...], rsum[...], NT, precision=HI, preferred_element_type=F32)
        right = right * (1.0 / replicas)
        qt[...] = right
        zturn = lax.dot_general(right, inv[...], TN, precision=HI, preferred_element_type=F32)
        zhi[...], zlo[...] = halves(zturn)

    pt = halves(ordered(spots[2], mine, theirs))
    approx = dot3((zhi[...], zlo[...]), pt, NN)
    update[...] = approx.astype(BF16).T
    newfb[...] = (merged[...] - approx).astype(BF16).T


def final(spots, inv, rsum, mine, theirs, merged, replicas):
    width = merged.shape[1]
    half = RANK // 2
    return pl.pallas_call(
        lambda *refs: final_kernel(replicas, *refs),
        grid=(width // WIDE,),
        in_specs=[
            SMEM_SPEC,
            whole_spec(RANK, RANK),
            whole_spec(HD, RANK),
            cols_spec(half, WIDE),
            cols_spec(half, WIDE),
            cols_spec(HD, WIDE),
        ],
        out_specs=[whole_spec(RANK, HD), rows_spec(WIDE, HD), rows_spec(WIDE, HD)],
        out_shape=[
            jax.ShapeDtypeStruct((RANK, HD), F32),
            jax.ShapeDtypeStruct((width, HD), BF16),
            jax.ShapeDtypeStruct((width, HD), BF16),
        ],
        scratch_shapes=[pltpu.VMEM((HD, RANK), BF16)] * 2,
        cost_estimate=cost(6 * width * RANK * HD, 12 * width * HD),
        name="final",
    )(spots, inv, rsum, mine, theirs, merged)


def tied(arrays, others):
    return lax.optimization_barrier((arrays, others))[0]


def neighbours(block, step):
    return step(block, 1), step(block, -1)


def to_pass_on(before, after):
    rows = before.shape[0]
    return before[: rows // 2], after[rows // 2 :]


def gather_line(block, before, after, passed, step):
    return block, after, step(passed[0], 1), step(passed[1], -1), before


def scatter_near(up, down, step):
    return step(up, 1), step(down, -1)


def scatter_far(got_up, got_down, rest, step):
    mid = rest.shape[0] // 2
    low = lambda array: array[:mid].astype(F32)
    high = lambda array: array[mid:].astype(F32)
    sum_up = step((low(rest) + low(got_up)).astype(BF16), 1)
    sum_down = step((high(rest) + high(got_down)).astype(BF16), -1)
    return got_up, got_down, sum_up, sum_down


def sum_left(keep, give):
    chip = (keep + other_core(give)).astype(BF16)
    mid = chip.shape[0] // 2
    near = lambda array: along_dp(array, lambda x, c: (x ^ 1, c))
    far = lambda array: along_dp(array, lambda x, c: (3 - x, c))
    add = lambda a, b: a.astype(F32) + b.astype(F32)
    first, second = chip[:mid], chip[mid:]
    first_pair = add(first, near(first)).astype(BF16)
    second_pair = add(second, far(second)).astype(BF16)
    mine = jnp.concatenate(
        [add(first_pair, far(first_pair)), add(second_pair, near(second_pair))], axis=0
    )
    return mine, other_core(mine)


def sum_right(part):
    chip = part + other_core(part)
    ahead = along_dp(chip, lambda x, c: (x + 1, c))
    behind = along_dp(chip, lambda x, c: (x - 1, c))
    across = along_dp(chip, lambda x, c: (x + 2, c))
    return (chip + across) + (ahead + behind)


def local(acts, cot_kv, w_kv, feedback, q_init):
    tokens, width = acts.shape
    half = width // 2
    replicas = lax.axis_size("dp")
    place = lax.axis_index("dp")
    core = place % 2
    spot = lax.axis_index("tensor")
    z, y = spot // SIDE, spot % SIDE
    spots = jnp.stack([z, y, core]).astype(jnp.int32)
    in_y = lambda array, k: along_tensor(array, 0, k)
    in_z = lambda array, k: along_tensor(array, k, 0)
    lines_z = [[z * SIDE + y for z in range(SIDE)] for y in range(SIDE)]
    lines_y = [[z * SIDE + y for y in range(SIDE)] for z in range(SIDE)]
    flat = SIDE * tokens

    blocks = acts[:, :half], acts[:, half:]
    near = neighbours(blocks[0], in_y)
    cots = lax.all_to_all(
        cot_kv, "tensor", 0, 0, axis_index_groups=lines_z, tiled=True
    ).reshape(SIDE, flat, HD)
    share = lax.dynamic_slice(w_kv, (core * half, 0), (half, HD))
    weights = lax.all_gather(share, "tensor", axis=0, axis_index_groups=lines_z)

    fb_turned = feedback.T
    qcols = q_init.T
    qrows = jnp.where(
        core == 0, qcols, jnp.concatenate([qcols[RANK // 2 :], qcols[: RANK // 2]], axis=0)
    )
    near, fb_turned, qrows, cots = lax.optimization_barrier((near, fb_turned, qrows, cots))
    cturn = turn_cots(spots, cots)
    pieces = gather_line(blocks[0], *near, to_pass_on(*near), in_y)
    near = neighbours(tied(blocks[1], pieces), in_y)
    own_a, up, down, rest_a = grad_parts(pieces, cturn)
    got_a = scatter_near(up, down, in_z)
    near, up = lax.optimization_barrier((near, up))
    passed = tied(to_pass_on(*near), got_a)
    pieces = gather_line(blocks[1], *near, passed, in_y)

    weights = tied(weights, (near, got_a))
    shares = input_parts(spots, (weights, other_core(weights)), cots)
    sums_a = scatter_far(*got_a, rest_a, in_z)

    pieces, sums_a, shares = lax.optimization_barrier((pieces, sums_a, shares))
    own_b, up, down, rest_b = grad_parts(pieces, cturn)
    got_b = scatter_near(up, down, in_z)
    input_grad = lax.psum_scatter(
        tied(shares, up), "tensor", scatter_dimension=0, axis_index_groups=lines_y, tiled=True
    )

    left = merge(fb_turned, own_a, tied(sums_a, got_b), qrows, 0, ())
    sums_b = scatter_far(*got_b, rest_b, in_z)
    sums_b, left = lax.optimization_barrier((sums_b, left))
    merged, keep, give = merge(fb_turned, own_b, sums_b, qrows, 1, left)
    mine, theirs = sum_left(keep, give)
    right, gram = gram_of(spots, mine, theirs, merged)
    inv = inverse_factor(gram)
    rsum = sum_right(right)
    qt, update, new_feedback = final(spots, inv, rsum, mine, theirs, merged, replicas)
    return input_grad, update, qt.T, new_feedback


def solution(mesh):
    placed = (
        P(("dp", "tensor"), None),
        P("dp", "tensor"),
        P(None, "tensor"),
        P("dp", "tensor"),
        P("tensor", None),
    )
    return jax.shard_map(
        local,
        mesh=mesh,
        in_specs=placed,
        out_specs=(
            P(("dp", "tensor"), None),
            P(None, "tensor"),
            P("tensor", None),
            P("dp", "tensor"),
        ),
        check_vma=False,
    )
```

```python
import jax
import jax.numpy as jnp
from jax import lax
from jax.experimental import pallas as pl
from jax.experimental.pallas import tpu as pltpu
from jax.sharding import PartitionSpec as P

HD = 128
RANK = 64
SIDE = 4
TILE = 2048
WIDE = 2048
LONG = 4096
VMEM = 40 * 1024 * 1024
PART = 1024
F32 = jnp.float32
BF16 = jnp.bfloat16
HI = lax.Precision.HIGHEST
NN = (((1,), (0,)), ((), ()))
NT = (((1,), (1,)), ((), ()))
TN = (((0,), (0,)), ((), ()))


def along_tensor(array, dz, dy):
    perm = [
        (z * SIDE + y, (z + dz) % SIDE * SIDE + (y + dy) % SIDE)
        for z in range(SIDE)
        for y in range(SIDE)
    ]
    return lax.ppermute(array, "tensor", perm)


def along_dp(array, target):
    perm = []
    for x in range(SIDE):
        for c in range(2):
            to_x, to_c = target(x, c)
            perm.append((x * 2 + c, to_x % SIDE * 2 + to_c))
    return lax.ppermute(array, "dp", perm)


def other_core(array):
    return along_dp(array, lambda x, c: (x, 1 - c))


def cost(flops, moved):
    return pl.CostEstimate(flops=int(flops), bytes_accessed=int(moved), transcendentals=0)


def cols_spec(rows, cols):
    return pl.BlockSpec((rows, cols), lambda j: (0, j))


def rows_spec(rows, cols):
    return pl.BlockSpec((rows, cols), lambda j: (j, 0))


def whole_spec(rows, cols):
    return pl.BlockSpec((rows, cols), lambda j: (0, 0))


ANY_SPEC = pl.BlockSpec(memory_space=pl.ANY)
SMEM_SPEC = pl.BlockSpec(memory_space=pltpu.SMEM)


def halves(array):
    high = array.astype(BF16)
    return high, (array - high.astype(F32)).astype(BF16)


def dot3(left, right, dims):
    dot = lambda a, b: lax.dot_general(a, b, dims, preferred_element_type=F32)
    return dot(left[0], right[0]) + (dot(left[0], right[1]) + dot(left[1], right[0]))


def turn_kernel(spots, cots, cturn):
    for r in range(SIDE):
        block = cots.at[(spots[0] + r) % SIDE]
        for s in range(SIDE):
            rows = pl.ds(pl.multiple_of((spots[1] + s) % SIDE * HD, HD), HD)
            cturn[r * HD : (r + 1) * HD, s * HD : (s + 1) * HD] = block[rows, :].T


def turn_cots(spots, cots):
    flat = cots.shape[1]
    return pl.pallas_call(
        turn_kernel,
        in_specs=[SMEM_SPEC, pl.BlockSpec(memory_space=pltpu.VMEM)],
        out_specs=pl.BlockSpec(memory_space=pltpu.VMEM),
        out_shape=jax.ShapeDtypeStruct((SIDE * HD, flat), BF16),
        cost_estimate=cost(0, 4 * SIDE * HD * flat),
        name="turn_cots",
    )(spots, cots)


def own_kernel(a0, a1, a2lo, a2hi, a3, cturn, own):
    tokens = jnp.concatenate([a0[...], a1[...], a2lo[...], a2hi[...], a3[...]], axis=0)
    own[...] = lax.dot_general(cturn[:HD], tokens, NN, preferred_element_type=F32)


def own_part(pieces, cturn):
    rows, width = pieces[0].shape
    flat = SIDE * rows
    return pl.pallas_call(
        own_kernel,
        grid=(width // TILE,),
        in_specs=[cols_spec(piece.shape[0], TILE) for piece in pieces] + [whole_spec(HD, flat)],
        out_specs=cols_spec(HD, TILE),
        out_shape=jax.ShapeDtypeStruct((HD, width), F32),
        cost_estimate=cost(2 * width * flat * HD, 12 * width * HD),
        name="own_part",
    )(*pieces, cturn)


def grad_kernel(a0, a1, a2lo, a2hi, a3, cturn, up, down, rest):
    j = pl.program_id(0)
    mid = pl.num_programs(0) // 2
    tokens = jnp.concatenate([a0[...], a1[...], a2lo[...], a2hi[...], a3[...]], axis=0)
    grads = lax.dot_general(cturn[HD:], tokens, NN, preferred_element_type=F32)
    ahead = grads[:HD].astype(BF16)
    across = grads[HD : 2 * HD].astype(BF16)
    behind = grads[2 * HD :].astype(BF16)

    @pl.when(j < mid)
    def _():
        up[...] = across
        down[...] = behind
        rest[...] = ahead

    @pl.when(j >= mid)
    def _():
        up[...] = ahead
        down[...] = across
        rest[...] = behind


def grad_parts(pieces, cturn):
    rows, width = pieces[0].shape
    flat = SIDE * rows
    mid = width // TILE // 2
    stacked = pl.BlockSpec((HD, TILE), lambda j: (j // mid, j % mid))
    return pl.pallas_call(
        grad_kernel,
        grid=(width // TILE,),
        in_specs=[cols_spec(piece.shape[0], TILE) for piece in pieces]
        + [whole_spec(SIDE * HD, flat)],
        out_specs=[stacked] * 3,
        out_shape=[jax.ShapeDtypeStruct((2 * HD, width // 2), BF16)] * 3,
        cost_estimate=cost(2 * width * SIDE * flat * HD, 9 * width * HD * 2),
        name="grad_parts",
    )(*pieces, cturn)


def input_product(mine, theirs, cots):
    first = pl.program_id(0) < pl.num_programs(0) // 2
    weights = jnp.concatenate(
        [jnp.where(first, mine[k], theirs[k]) for k in range(SIDE)], axis=1
    )
    return lax.dot_general(cots, weights, NT, preferred_element_type=F32)


def input_kernel(spots, mine, theirs, cots, out):
    lined = jnp.concatenate([cots[k] for k in range(SIDE)], axis=1)
    out[...] = input_product(mine, theirs, lined).astype(BF16)


def input_parts(spots, gathered, cots):
    piece = gathered[0].shape[1]
    flat = cots.shape[1]
    mid = piece // PART
    place = lambda j, spots: (spots[2] + j // mid) % 2 * mid + j % mid
    return pl.pallas_call(
        input_kernel,
        grid_spec=pltpu.PrefetchScalarGridSpec(
            num_scalar_prefetch=1,
            grid=(2 * mid,),
            in_specs=[
                pl.BlockSpec((SIDE, PART, HD), lambda j, spots: (0, jnp.minimum(j, mid - 1), 0)),
                pl.BlockSpec((SIDE, PART, HD), lambda j, spots: (0, jnp.maximum(j - mid, 0), 0)),
                pl.BlockSpec((SIDE, flat, HD), lambda j, spots: (0, 0, 0)),
            ],
            out_specs=pl.BlockSpec((flat, PART), lambda j, spots: (0, place(j, spots))),
        ),
        out_shape=jax.ShapeDtypeStruct((flat, 2 * piece), BF16),
        cost_estimate=cost(4 * piece * SIDE * flat * HD, 18 * piece * HD * 2),
        name="input_parts",
    )(spots, *gathered, cots)


def merge_kernel(fb, own, pl_lo, pl_hi, su_lo, su_hi, qrows, *refs):
    merged, keep, give = refs[-3:]
    j = pl.program_id(0)
    mid = pl.num_programs(0) // 2
    base = fb[...].astype(F32) + own[...]

    def finish(plain, summed):
        total = base + (plain[...].astype(F32) + summed[...].astype(F32))
        merged[...] = total
        share = dot3(halves(qrows[...]), halves(total), NN)
        keep[...] = share[: RANK // 2]
        give[...] = share[RANK // 2 :]

    @pl.when(j < mid)
    def _():
        finish(pl_lo, su_lo)

    @pl.when(j >= mid)
    def _():
        finish(pl_hi, su_hi)


def merge(feedback, own, sums, qrows, part, before):
    got_up, got_down, sum_up, sum_down = sums
    width = own.shape[1]
    steps = width // WIDE
    mid = steps // 2
    first = part * steps
    shifted = lambda rows: pl.BlockSpec((rows, WIDE), lambda j: (0, first + j))
    low = pl.BlockSpec((HD, WIDE), lambda j: (0, jnp.minimum(j, mid - 1)))
    high = pl.BlockSpec((HD, WIDE), lambda j: (1, jnp.maximum(j - mid, 0)))
    high_from = pl.BlockSpec((HD, WIDE), lambda j: (0, jnp.maximum(j - mid, 0)))
    return pl.pallas_call(
        merge_kernel,
        grid=(steps,),
        in_specs=[shifted(HD), cols_spec(HD, WIDE), low, high, low, high_from, whole_spec(RANK, HD)]
        + [ANY_SPEC] * len(before),
        out_specs=[shifted(HD), shifted(RANK // 2), shifted(RANK // 2)],
        out_shape=[
            jax.ShapeDtypeStruct((HD, 2 * width), F32),
            jax.ShapeDtypeStruct((RANK // 2, 2 * width), F32),
            jax.ShapeDtypeStruct((RANK // 2, 2 * width), F32),
        ],
        input_output_aliases={7 + k: k for k in range(len(before))},
        cost_estimate=cost(6 * width * RANK * HD, 14 * width * HD),
        name="merge",
    )(feedback, own, got_down, got_up, sum_up, sum_down, qrows, *before)


def ordered(core, mine, theirs):
    first = jnp.where(core == 0, mine[...], theirs[...])
    second = jnp.where(core == 0, theirs[...], mine[...])
    return jnp.concatenate([first, second], axis=0)


def gram_kernel(spots, mine, theirs, merged, right, gram):
    @pl.when(pl.program_id(0) == 0)
    def _():
        gram[...] = jnp.zeros_like(gram)
        right[...] = jnp.zeros_like(right)

    pt = halves(ordered(spots[2], mine, theirs))
    right[...] += dot3(halves(merged[...]), pt, NT)
    gram[...] += dot3(pt, pt, NT)


def gram_of(spots, mine, theirs, merged):
    width = merged.shape[1]
    half = RANK // 2
    return pl.pallas_call(
        gram_kernel,
        grid=(width // LONG,),
        in_specs=[SMEM_SPEC, cols_spec(half, LONG), cols_spec(half, LONG), cols_spec(HD, LONG)],
        out_specs=[whole_spec(HD, RANK), whole_spec(RANK, RANK)],
        out_shape=[
            jax.ShapeDtypeStruct((HD, RANK), F32),
            jax.ShapeDtypeStruct((RANK, RANK), F32),
        ],
        cost_estimate=cost(6 * width * RANK * (RANK + HD), 6 * width * HD),
        compiler_params=pltpu.CompilerParams(vmem_limit_bytes=VMEM),
        name="gram",
    )(spots, mine, theirs, merged)


def inverse_kernel(gram, out):
    row = lax.broadcasted_iota(jnp.int32, (RANK, RANK), 0)
    col = lax.broadcasted_iota(jnp.int32, (RANK, RANK), 1)
    eye = jnp.where(row == col, 1.0, 0.0).astype(F32)
    mat = jnp.concatenate([gram[...], eye], axis=1)
    below = lax.broadcasted_iota(jnp.int32, (RANK, 1), 0)
    for k in range(RANK - 1):
        pivot = mat[k : k + 1, :]
        column = mat[:, k : k + 1]
        factor = jnp.where(below > k, column / mat[k : k + 1, k : k + 1], 0.0)
        mat = mat - factor * pivot
    diag = jnp.sum(jnp.where(row == col, mat[:, :RANK], 0.0), axis=1, keepdims=True)
    out[...] = mat[:, RANK:] / jnp.sqrt(diag)


def inverse_factor(gram):
    return pl.pallas_call(
        inverse_kernel,
        out_shape=jax.ShapeDtypeStruct((RANK, RANK), F32),
        cost_estimate=cost(RANK * RANK * RANK * 400, RANK * RANK * 16),
        name="inverse_factor",
    )(gram)


def final_kernel(replicas, spots, inv, rsum, mine, theirs, merged, qt, update, newfb, zhi, zlo):
    @pl.when(pl.program_id(0) == 0)
    def _():
        right = lax.dot_general(inv[...], rsum[...], NT, precision=HI, preferred_element_type=F32)
        right = right * (1.0 / replicas)
        qt[...] = right
        zturn = lax.dot_general(right, inv[...], TN, precision=HI, preferred_element_type=F32)
        zhi[...], zlo[...] = halves(zturn)

    pt = halves(ordered(spots[2], mine, theirs))
    approx = dot3((zhi[...], zlo[...]), pt, NN)
    update[...] = approx.astype(BF16).T
    newfb[...] = (merged[...] - approx).astype(BF16).T


def final(spots, inv, rsum, mine, theirs, merged, replicas):
    width = merged.shape[1]
    half = RANK // 2
    return pl.pallas_call(
        lambda *refs: final_kernel(replicas, *refs),
        grid=(width // WIDE,),
        in_specs=[
            SMEM_SPEC,
            whole_spec(RANK, RANK),
            whole_spec(HD, RANK),
            cols_spec(half, WIDE),
            cols_spec(half, WIDE),
            cols_spec(HD, WIDE),
        ],
        out_specs=[whole_spec(RANK, HD), rows_spec(WIDE, HD), rows_spec(WIDE, HD)],
        out_shape=[
            jax.ShapeDtypeStruct((RANK, HD), F32),
            jax.ShapeDtypeStruct((width, HD), BF16),
            jax.ShapeDtypeStruct((width, HD), BF16),
        ],
        scratch_shapes=[pltpu.VMEM((HD, RANK), BF16)] * 2,
        cost_estimate=cost(6 * width * RANK * HD, 12 * width * HD),
        name="final",
    )(spots, inv, rsum, mine, theirs, merged)


def tied(arrays, others):
    return lax.optimization_barrier((arrays, others))[0]


def neighbours(block, step):
    return step(block, 1), step(block, -1)


def to_pass_on(before, after):
    rows = before.shape[0]
    return before[: rows // 2], after[rows // 2 :]


def gather_line(block, before, after, passed, step):
    return block, after, step(passed[0], 1), step(passed[1], -1), before


def scatter_near(up, down, step):
    return step(up, 1), step(down, -1)


def scatter_far(got_up, got_down, rest, step):
    mid = rest.shape[0] // 2
    low = lambda array: array[:mid].astype(F32)
    high = lambda array: array[mid:].astype(F32)
    sum_up = step((low(rest) + low(got_up)).astype(BF16), 1)
    sum_down = step((high(rest) + high(got_down)).astype(BF16), -1)
    return got_up, got_down, sum_up, sum_down


def sum_left(keep, give):
    chip = (keep + other_core(give)).astype(BF16)
    mid = chip.shape[0] // 2
    near = lambda array: along_dp(array, lambda x, c: (x ^ 1, c))
    far = lambda array: along_dp(array, lambda x, c: (3 - x, c))
    add = lambda a, b: a.astype(F32) + b.astype(F32)
    first, second = chip[:mid], chip[mid:]
    first_pair = add(first, near(first)).astype(BF16)
    second_pair = add(second, far(second)).astype(BF16)
    mine = jnp.concatenate(
        [add(first_pair, far(first_pair)), add(second_pair, near(second_pair))], axis=0
    )
    return mine, other_core(mine)


def sum_right(part):
    chip = part + other_core(part)
    ahead = along_dp(chip, lambda x, c: (x + 1, c))
    behind = along_dp(chip, lambda x, c: (x - 1, c))
    across = along_dp(chip, lambda x, c: (x + 2, c))
    return (chip + across) + (ahead + behind)


def local(acts, cot_kv, w_kv, feedback, q_init):
    tokens, width = acts.shape
    half = width // 2
    replicas = lax.axis_size("dp")
    place = lax.axis_index("dp")
    core = place % 2
    spot = lax.axis_index("tensor")
    z, y = spot // SIDE, spot % SIDE
    spots = jnp.stack([z, y, core]).astype(jnp.int32)
    in_y = lambda array, k: along_tensor(array, 0, k)
    in_z = lambda array, k: along_tensor(array, k, 0)
    lines_z = [[z * SIDE + y for z in range(SIDE)] for y in range(SIDE)]
    lines_y = [[z * SIDE + y for y in range(SIDE)] for z in range(SIDE)]
    flat = SIDE * tokens

    blocks = acts[:, :half], acts[:, half:]
    near = neighbours(blocks[0], in_y)
    cots = lax.all_to_all(
        cot_kv, "tensor", 0, 0, axis_index_groups=lines_z, tiled=True
    ).reshape(SIDE, flat, HD)
    share = lax.dynamic_slice(w_kv, (core * half, 0), (half, HD))
    weights = lax.all_gather(share, "tensor", axis=0, axis_index_groups=lines_z)

    fb_turned = feedback.T
    qcols = q_init.T
    qrows = jnp.where(
        core == 0, qcols, jnp.concatenate([qcols[RANK // 2 :], qcols[: RANK // 2]], axis=0)
    )
    near, fb_turned, qrows, cots = lax.optimization_barrier((near, fb_turned, qrows, cots))
    cturn = turn_cots(spots, cots)
    pieces = gather_line(blocks[0], *near, to_pass_on(*near), in_y)
    near = neighbours(tied(blocks[1], pieces), in_y)
    up, down, rest_a = grad_parts(pieces, cturn)
    pieces_a = pieces
    got_a = scatter_near(up, down, in_z)
    near, up = lax.optimization_barrier((near, up))
    passed = tied(to_pass_on(*near), got_a)
    pieces = gather_line(blocks[1], *near, passed, in_y)

    weights = tied(weights, (near, got_a))
    shares = input_parts(spots, (weights, other_core(weights)), cots)
    sums_a = scatter_far(*got_a, rest_a, in_z)

    pieces, sums_a, shares = lax.optimization_barrier((pieces, sums_a, shares))
    up, down, rest_b = grad_parts(pieces, cturn)
    later, up = lax.optimization_barrier(((pieces_a, pieces), up))
    own_a, own_b = own_part(later[0], cturn), own_part(later[1], cturn)
    got_b = scatter_near(up, down, in_z)
    input_grad = lax.psum_scatter(
        tied(shares, up), "tensor", scatter_dimension=0, axis_index_groups=lines_y, tiled=True
    )

    got_b, own_a, own_b = lax.optimization_barrier((got_b, own_a, own_b))
    left = merge(fb_turned, own_a, tied(sums_a, got_b), qrows, 0, ())
    sums_b = scatter_far(*got_b, rest_b, in_z)
    sums_b, left = lax.optimization_barrier((sums_b, left))
    merged, keep, give = merge(fb_turned, own_b, sums_b, qrows, 1, left)
    mine, theirs = sum_left(keep, give)
    right, gram = gram_of(spots, mine, theirs, merged)
    inv = inverse_factor(gram)
    rsum = sum_right(right)
    qt, update, new_feedback = final(spots, inv, rsum, mine, theirs, merged, replicas)
    return input_grad, update, qt.T, new_feedback


def solution(mesh):
    placed = (
        P(("dp", "tensor"), None),
        P("dp", "tensor"),
        P(None, "tensor"),
        P("dp", "tensor"),
        P("tensor", None),
    )
    return jax.shard_map(
        local,
        mesh=mesh,
        in_specs=placed,
        out_specs=(
            P(("dp", "tensor"), None),
            P(None, "tensor"),
            P("tensor", None),
            P("dp", "tensor"),
        ),
        check_vma=False,
    )
```

```python
import jax
import jax.numpy as jnp
from jax import lax
from jax.experimental import pallas as pl
from jax.experimental.pallas import tpu as pltpu
from jax.sharding import PartitionSpec as P

HD = 128
RANK = 64
SIDE = 4
TILE = 2048
WIDE = 2048
LONG = 4096
VMEM = 40 * 1024 * 1024
PART = 1024
F32 = jnp.float32
BF16 = jnp.bfloat16
HI = lax.Precision.HIGHEST
NN = (((1,), (0,)), ((), ()))
NT = (((1,), (1,)), ((), ()))
TN = (((0,), (0,)), ((), ()))


def along_tensor(array, dz, dy):
    perm = [
        (z * SIDE + y, (z + dz) % SIDE * SIDE + (y + dy) % SIDE)
        for z in range(SIDE)
        for y in range(SIDE)
    ]
    return lax.ppermute(array, "tensor", perm)


def along_dp(array, target):
    perm = []
    for x in range(SIDE):
        for c in range(2):
            to_x, to_c = target(x, c)
            perm.append((x * 2 + c, to_x % SIDE * 2 + to_c))
    return lax.ppermute(array, "dp", perm)


def other_core(array):
    return along_dp(array, lambda x, c: (x, 1 - c))


def cost(flops, moved):
    return pl.CostEstimate(flops=int(flops), bytes_accessed=int(moved), transcendentals=0)


def cols_spec(rows, cols):
    return pl.BlockSpec((rows, cols), lambda j: (0, j))


def rows_spec(rows, cols):
    return pl.BlockSpec((rows, cols), lambda j: (j, 0))


def whole_spec(rows, cols):
    return pl.BlockSpec((rows, cols), lambda j: (0, 0))


ANY_SPEC = pl.BlockSpec(memory_space=pl.ANY)
SMEM_SPEC = pl.BlockSpec(memory_space=pltpu.SMEM)


def halves(array):
    high = array.astype(BF16)
    return high, (array - high.astype(F32)).astype(BF16)


def dot3(left, right, dims):
    dot = lambda a, b: lax.dot_general(a, b, dims, preferred_element_type=F32)
    return dot(left[0], right[0]) + (dot(left[0], right[1]) + dot(left[1], right[0]))


def dot2(left, right, dims):
    dot = lambda a: lax.dot_general(a, right, dims, preferred_element_type=F32)
    return dot(left[0]) + dot(left[1])


def turn_kernel(spots, cots, cturn):
    for r in range(SIDE):
        block = cots.at[(spots[0] + r) % SIDE]
        for s in range(SIDE):
            rows = pl.ds(pl.multiple_of((spots[1] + s) % SIDE * HD, HD), HD)
            cturn[r * HD : (r + 1) * HD, s * HD : (s + 1) * HD] = block[rows, :].T


def turn_cots(spots, cots):
    flat = cots.shape[1]
    return pl.pallas_call(
        turn_kernel,
        in_specs=[SMEM_SPEC, pl.BlockSpec(memory_space=pltpu.VMEM)],
        out_specs=pl.BlockSpec(memory_space=pltpu.VMEM),
        out_shape=jax.ShapeDtypeStruct((SIDE * HD, flat), BF16),
        cost_estimate=cost(0, 4 * SIDE * HD * flat),
        name="turn_cots",
    )(spots, cots)


def own_kernel(a0, a1, a2lo, a2hi, a3, cturn, own):
    tokens = jnp.concatenate([a0[...], a1[...], a2lo[...], a2hi[...], a3[...]], axis=0)
    own[...] = lax.dot_general(cturn[:HD], tokens, NN, preferred_element_type=F32)


def own_part(pieces, cturn):
    rows, width = pieces[0].shape
    flat = SIDE * rows
    return pl.pallas_call(
        own_kernel,
        grid=(width // TILE,),
        in_specs=[cols_spec(piece.shape[0], TILE) for piece in pieces] + [whole_spec(HD, flat)],
        out_specs=cols_spec(HD, TILE),
        out_shape=jax.ShapeDtypeStruct((HD, width), F32),
        cost_estimate=cost(2 * width * flat * HD, 12 * width * HD),
        name="own_part",
    )(*pieces, cturn)


def grad_kernel(a0, a1, a2lo, a2hi, a3, cturn, up, down, rest):
    j = pl.program_id(0)
    mid = pl.num_programs(0) // 2
    tokens = jnp.concatenate([a0[...], a1[...], a2lo[...], a2hi[...], a3[...]], axis=0)
    grads = lax.dot_general(cturn[HD:], tokens, NN, preferred_element_type=F32)
    ahead = grads[:HD].astype(BF16)
    across = grads[HD : 2 * HD].astype(BF16)
    behind = grads[2 * HD :].astype(BF16)

    @pl.when(j < mid)
    def _():
        up[...] = across
        down[...] = behind
        rest[...] = ahead

    @pl.when(j >= mid)
    def _():
        up[...] = ahead
        down[...] = across
        rest[...] = behind


def grad_parts(pieces, cturn):
    rows, width = pieces[0].shape
    flat = SIDE * rows
    mid = width // TILE // 2
    stacked = pl.BlockSpec((HD, TILE), lambda j: (j // mid, j % mid))
    return pl.pallas_call(
        grad_kernel,
        grid=(width // TILE,),
        in_specs=[cols_spec(piece.shape[0], TILE) for piece in pieces]
        + [whole_spec(SIDE * HD, flat)],
        out_specs=[stacked] * 3,
        out_shape=[jax.ShapeDtypeStruct((2 * HD, width // 2), BF16)] * 3,
        cost_estimate=cost(2 * width * SIDE * flat * HD, 9 * width * HD * 2),
        name="grad_parts",
    )(*pieces, cturn)


def input_product(mine, theirs, cots):
    first = pl.program_id(0) < pl.num_programs(0) // 2
    weights = jnp.concatenate(
        [jnp.where(first, mine[k], theirs[k]) for k in range(SIDE)], axis=1
    )
    return lax.dot_general(cots, weights, NT, preferred_element_type=F32)


def input_kernel(spots, mine, theirs, cots, out):
    lined = jnp.concatenate([cots[k] for k in range(SIDE)], axis=1)
    out[...] = input_product(mine, theirs, lined).astype(BF16)


def input_parts(spots, gathered, cots):
    piece = gathered[0].shape[1]
    flat = cots.shape[1]
    mid = piece // PART
    place = lambda j, spots: (spots[2] + j // mid) % 2 * mid + j % mid
    return pl.pallas_call(
        input_kernel,
        grid_spec=pltpu.PrefetchScalarGridSpec(
            num_scalar_prefetch=1,
            grid=(2 * mid,),
            in_specs=[
                pl.BlockSpec((SIDE, PART, HD), lambda j, spots: (0, jnp.minimum(j, mid - 1), 0)),
                pl.BlockSpec((SIDE, PART, HD), lambda j, spots: (0, jnp.maximum(j - mid, 0), 0)),
                pl.BlockSpec((SIDE, flat, HD), lambda j, spots: (0, 0, 0)),
            ],
            out_specs=pl.BlockSpec((flat, PART), lambda j, spots: (0, place(j, spots))),
        ),
        out_shape=jax.ShapeDtypeStruct((flat, 2 * piece), BF16),
        cost_estimate=cost(4 * piece * SIDE * flat * HD, 18 * piece * HD * 2),
        name="input_parts",
    )(spots, *gathered, cots)


def merge_kernel(fb, own, pl_lo, pl_hi, su_lo, su_hi, qrows, *refs):
    merged, keep, give = refs[-3:]
    j = pl.program_id(0)
    mid = pl.num_programs(0) // 2
    base = fb[...].astype(F32) + own[...]

    def finish(plain, summed):
        total = base + (plain[...].astype(F32) + summed[...].astype(F32))
        merged[...] = total
        share = dot3(halves(qrows[...]), halves(total), NN)
        keep[...] = share[: RANK // 2]
        give[...] = share[RANK // 2 :].astype(BF16)

    @pl.when(j < mid)
    def _():
        finish(pl_lo, su_lo)

    @pl.when(j >= mid)
    def _():
        finish(pl_hi, su_hi)


def merge(feedback, own, sums, qrows, part, before):
    got_up, got_down, sum_up, sum_down = sums
    width = own.shape[1]
    steps = width // WIDE
    mid = steps // 2
    first = part * steps
    shifted = lambda rows: pl.BlockSpec((rows, WIDE), lambda j: (0, first + j))
    low = pl.BlockSpec((HD, WIDE), lambda j: (0, jnp.minimum(j, mid - 1)))
    high = pl.BlockSpec((HD, WIDE), lambda j: (1, jnp.maximum(j - mid, 0)))
    high_from = pl.BlockSpec((HD, WIDE), lambda j: (0, jnp.maximum(j - mid, 0)))
    return pl.pallas_call(
        merge_kernel,
        grid=(steps,),
        in_specs=[shifted(HD), cols_spec(HD, WIDE), low, high, low, high_from, whole_spec(RANK, HD)]
        + [ANY_SPEC] * len(before),
        out_specs=[shifted(HD), shifted(RANK // 2), shifted(RANK // 2)],
        out_shape=[
            jax.ShapeDtypeStruct((HD, 2 * width), F32),
            jax.ShapeDtypeStruct((RANK // 2, 2 * width), F32),
            jax.ShapeDtypeStruct((RANK // 2, 2 * width), BF16),
        ],
        input_output_aliases={7 + k: k for k in range(len(before))},
        cost_estimate=cost(6 * width * RANK * HD, 14 * width * HD),
        name="merge",
    )(feedback, own, got_down, got_up, sum_up, sum_down, qrows, *before)


def ordered(core, mine, theirs):
    first = jnp.where(core == 0, mine[...], theirs[...])
    second = jnp.where(core == 0, theirs[...], mine[...])
    return jnp.concatenate([first, second], axis=0)


def gram_kernel(spots, mine, theirs, merged, right, gram):
    @pl.when(pl.program_id(0) == 0)
    def _():
        gram[...] = jnp.zeros_like(gram)
        right[...] = jnp.zeros_like(right)

    pt = ordered(spots[2], mine, theirs)
    right[...] += dot2(halves(merged[...]), pt, NT)
    gram[...] += lax.dot_general(pt, pt, NT, preferred_element_type=F32)


def gram_of(spots, mine, theirs, merged):
    width = merged.shape[1]
    half = RANK // 2
    return pl.pallas_call(
        gram_kernel,
        grid=(width // LONG,),
        in_specs=[SMEM_SPEC, cols_spec(half, LONG), cols_spec(half, LONG), cols_spec(HD, LONG)],
        out_specs=[whole_spec(HD, RANK), whole_spec(RANK, RANK)],
        out_shape=[
            jax.ShapeDtypeStruct((HD, RANK), F32),
            jax.ShapeDtypeStruct((RANK, RANK), F32),
        ],
        cost_estimate=cost(6 * width * RANK * (RANK + HD), 6 * width * HD),
        compiler_params=pltpu.CompilerParams(vmem_limit_bytes=VMEM),
        name="gram",
    )(spots, mine, theirs, merged)


def inverse_kernel(gram, out):
    row = lax.broadcasted_iota(jnp.int32, (RANK, RANK), 0)
    col = lax.broadcasted_iota(jnp.int32, (RANK, RANK), 1)
    eye = jnp.where(row == col, 1.0, 0.0).astype(F32)
    mat = jnp.concatenate([gram[...], eye], axis=1)
    below = lax.broadcasted_iota(jnp.int32, (RANK, 1), 0)
    for k in range(RANK - 1):
        pivot = mat[k : k + 1, :]
        column = mat[:, k : k + 1]
        factor = jnp.where(below > k, column / mat[k : k + 1, k : k + 1], 0.0)
        mat = mat - factor * pivot
    diag = jnp.sum(jnp.where(row == col, mat[:, :RANK], 0.0), axis=1, keepdims=True)
    out[...] = mat[:, RANK:] / jnp.sqrt(diag)


def inverse_factor(gram):
    return pl.pallas_call(
        inverse_kernel,
        out_shape=jax.ShapeDtypeStruct((RANK, RANK), F32),
        cost_estimate=cost(RANK * RANK * RANK * 400, RANK * RANK * 16),
        name="inverse_factor",
    )(gram)


def final_kernel(replicas, spots, inv, rsum, mine, theirs, merged, qt, update, newfb, zhi, zlo):
    @pl.when(pl.program_id(0) == 0)
    def _():
        right = lax.dot_general(inv[...], rsum[...], NT, precision=HI, preferred_element_type=F32)
        right = right * (1.0 / replicas)
        qt[...] = right
        zturn = lax.dot_general(right, inv[...], TN, precision=HI, preferred_element_type=F32)
        zhi[...], zlo[...] = halves(zturn)

    pt = ordered(spots[2], mine, theirs)
    approx = dot2((zhi[...], zlo[...]), pt, NN)
    update[...] = approx.astype(BF16).T
    newfb[...] = (merged[...] - approx).astype(BF16).T


def final(spots, inv, rsum, mine, theirs, merged, replicas):
    width = merged.shape[1]
    half = RANK // 2
    return pl.pallas_call(
        lambda *refs: final_kernel(replicas, *refs),
        grid=(width // WIDE,),
        in_specs=[
            SMEM_SPEC,
            whole_spec(RANK, RANK),
            whole_spec(HD, RANK),
            cols_spec(half, WIDE),
            cols_spec(half, WIDE),
            cols_spec(HD, WIDE),
        ],
        out_specs=[whole_spec(RANK, HD), rows_spec(WIDE, HD), rows_spec(WIDE, HD)],
        out_shape=[
            jax.ShapeDtypeStruct((RANK, HD), F32),
            jax.ShapeDtypeStruct((width, HD), BF16),
            jax.ShapeDtypeStruct((width, HD), BF16),
        ],
        scratch_shapes=[pltpu.VMEM((HD, RANK), BF16)] * 2,
        cost_estimate=cost(6 * width * RANK * HD, 12 * width * HD),
        name="final",
    )(spots, inv, rsum, mine, theirs, merged)


def tied(arrays, others):
    return lax.optimization_barrier((arrays, others))[0]


def neighbours(block, step):
    return step(block, 1), step(block, -1)


def to_pass_on(before, after):
    rows = before.shape[0]
    return before[: rows // 2], after[rows // 2 :]


def gather_line(block, before, after, passed, step):
    return block, after, step(passed[0], 1), step(passed[1], -1), before


def scatter_near(up, down, step):
    return step(up, 1), step(down, -1)


def scatter_far(got_up, got_down, rest, step):
    mid = rest.shape[0] // 2
    low = lambda array: array[:mid].astype(F32)
    high = lambda array: array[mid:].astype(F32)
    sum_up = step((low(rest) + low(got_up)).astype(BF16), 1)
    sum_down = step((high(rest) + high(got_down)).astype(BF16), -1)
    return got_up, got_down, sum_up, sum_down


def sum_left(keep, give):
    chip = (keep + other_core(give).astype(F32)).astype(BF16)
    mid = chip.shape[0] // 2
    near = lambda array: along_dp(array, lambda x, c: (x ^ 1, c))
    far = lambda array: along_dp(array, lambda x, c: (3 - x, c))
    add = lambda a, b: a.astype(F32) + b.astype(F32)
    first, second = chip[:mid], chip[mid:]
    first_pair = add(first, near(first)).astype(BF16)
    second_pair = add(second, far(second)).astype(BF16)
    mine = jnp.concatenate(
        [add(first_pair, far(first_pair)), add(second_pair, near(second_pair))], axis=0
    ).astype(BF16)
    return mine, other_core(mine)


def sum_right(part):
    chip = part + other_core(part)
    ahead = along_dp(chip, lambda x, c: (x + 1, c))
    behind = along_dp(chip, lambda x, c: (x - 1, c))
    across = along_dp(chip, lambda x, c: (x + 2, c))
    return (chip + across) + (ahead + behind)


def local(acts, cot_kv, w_kv, feedback, q_init):
    tokens, width = acts.shape
    half = width // 2
    replicas = lax.axis_size("dp")
    place = lax.axis_index("dp")
    core = place % 2
    spot = lax.axis_index("tensor")
    z, y = spot // SIDE, spot % SIDE
    spots = jnp.stack([z, y, core]).astype(jnp.int32)
    in_y = lambda array, k: along_tensor(array, 0, k)
    in_z = lambda array, k: along_tensor(array, k, 0)
    lines_z = [[z * SIDE + y for z in range(SIDE)] for y in range(SIDE)]
    lines_y = [[z * SIDE + y for y in range(SIDE)] for z in range(SIDE)]
    flat = SIDE * tokens

    blocks = acts[:, :half], acts[:, half:]
    near = neighbours(blocks[0], in_y)
    cots = lax.all_to_all(
        cot_kv, "tensor", 0, 0, axis_index_groups=lines_z, tiled=True
    ).reshape(SIDE, flat, HD)
    share = lax.dynamic_slice(w_kv, (core * half, 0), (half, HD))
    weights = lax.all_gather(share, "tensor", axis=0, axis_index_groups=lines_z)

    fb_turned = feedback.T
    qcols = q_init.T
    qrows = jnp.where(
        core == 0, qcols, jnp.concatenate([qcols[RANK // 2 :], qcols[: RANK // 2]], axis=0)
    )
    near, fb_turned, qrows, cots = lax.optimization_barrier((near, fb_turned, qrows, cots))
    cturn = turn_cots(spots, cots)
    pieces = gather_line(blocks[0], *near, to_pass_on(*near), in_y)
    near = neighbours(tied(blocks[1], pieces), in_y)
    up, down, rest_a = grad_parts(pieces, cturn)
    pieces_a = pieces
    got_a = scatter_near(up, down, in_z)
    near, up = lax.optimization_barrier((near, up))
    passed = tied(to_pass_on(*near), got_a)
    pieces = gather_line(blocks[1], *near, passed, in_y)

    weights = tied(weights, (near, got_a))
    shares = input_parts(spots, (weights, other_core(weights)), cots)
    sums_a = scatter_far(*got_a, rest_a, in_z)

    pieces, sums_a, shares = lax.optimization_barrier((pieces, sums_a, shares))
    up, down, rest_b = grad_parts(pieces, cturn)
    later, up = lax.optimization_barrier(((pieces_a, pieces), up))
    own_a, own_b = own_part(later[0], cturn), own_part(later[1], cturn)
    got_b = scatter_near(up, down, in_z)
    input_grad = lax.psum_scatter(
        tied(shares, up), "tensor", scatter_dimension=0, axis_index_groups=lines_y, tiled=True
    )

    got_b, own_a, own_b = lax.optimization_barrier((got_b, own_a, own_b))
    left = merge(fb_turned, own_a, tied(sums_a, got_b), qrows, 0, ())
    sums_b = scatter_far(*got_b, rest_b, in_z)
    sums_b, left = lax.optimization_barrier((sums_b, left))
    merged, keep, give = merge(fb_turned, own_b, sums_b, qrows, 1, left)
    mine, theirs = sum_left(keep, give)
    right, gram = gram_of(spots, mine, theirs, merged)
    inv = inverse_factor(gram)
    rsum = sum_right(right)
    qt, update, new_feedback = final(spots, inv, rsum, mine, theirs, merged, replicas)
    return input_grad, update, qt.T, new_feedback


def solution(mesh):
    placed = (
        P(("dp", "tensor"), None),
        P("dp", "tensor"),
        P(None, "tensor"),
        P("dp", "tensor"),
        P("tensor", None),
    )
    return jax.shard_map(
        local,
        mesh=mesh,
        in_specs=placed,
        out_specs=(
            P(("dp", "tensor"), None),
            P(None, "tensor"),
            P("tensor", None),
            P("dp", "tensor"),
        ),
        check_vma=False,
    )
```

```python
import jax
import jax.numpy as jnp
from jax import lax
from jax.experimental import pallas as pl
from jax.experimental.pallas import tpu as pltpu
from jax.sharding import PartitionSpec as P

HD = 128
RANK = 64
SIDE = 4
TILE = 2048
WIDE = 2048
LONG = 4096
VMEM = 24 * 1024 * 1024
PART = 2048
F32 = jnp.float32
BF16 = jnp.bfloat16
HI = lax.Precision.HIGHEST
NN = (((1,), (0,)), ((), ()))
NT = (((1,), (1,)), ((), ()))
TN = (((0,), (0,)), ((), ()))


def along_tensor(array, dz, dy):
    perm = [
        (z * SIDE + y, (z + dz) % SIDE * SIDE + (y + dy) % SIDE)
        for z in range(SIDE)
        for y in range(SIDE)
    ]
    return lax.ppermute(array, "tensor", perm)


def along_dp(array, target):
    perm = []
    for x in range(SIDE):
        for c in range(2):
            to_x, to_c = target(x, c)
            perm.append((x * 2 + c, to_x % SIDE * 2 + to_c))
    return lax.ppermute(array, "dp", perm)


def other_core(array):
    return along_dp(array, lambda x, c: (x, 1 - c))


def cost(flops, moved):
    return pl.CostEstimate(flops=int(flops), bytes_accessed=int(moved), transcendentals=0)


def cols_spec(rows, cols):
    return pl.BlockSpec((rows, cols), lambda j: (0, j))


def rows_spec(rows, cols):
    return pl.BlockSpec((rows, cols), lambda j: (j, 0))


def whole_spec(rows, cols):
    return pl.BlockSpec((rows, cols), lambda j: (0, 0))


ANY_SPEC = pl.BlockSpec(memory_space=pl.ANY)
SMEM_SPEC = pl.BlockSpec(memory_space=pltpu.SMEM)


def halves(array):
    high = array.astype(BF16)
    return high, (array - high.astype(F32)).astype(BF16)


def dot3(left, right, dims):
    dot = lambda a, b: lax.dot_general(a, b, dims, preferred_element_type=F32)
    return dot(left[0], right[0]) + (dot(left[0], right[1]) + dot(left[1], right[0]))


def dot2(left, right, dims):
    dot = lambda a: lax.dot_general(a, right, dims, preferred_element_type=F32)
    return dot(left[0]) + dot(left[1])


def turn_kernel(spots, cots, cturn):
    for r in range(SIDE):
        block = cots.at[(spots[0] + r) % SIDE]
        for s in range(SIDE):
            rows = pl.ds(pl.multiple_of((spots[1] + s) % SIDE * HD, HD), HD)
            cturn[r * HD : (r + 1) * HD, s * HD : (s + 1) * HD] = block[rows, :].T


def turn_cots(spots, cots):
    flat = cots.shape[1]
    return pl.pallas_call(
        turn_kernel,
        in_specs=[SMEM_SPEC, pl.BlockSpec(memory_space=pltpu.VMEM)],
        out_specs=pl.BlockSpec(memory_space=pltpu.VMEM),
        out_shape=jax.ShapeDtypeStruct((SIDE * HD, flat), BF16),
        cost_estimate=cost(0, 4 * SIDE * HD * flat),
        name="turn_cots",
    )(spots, cots)


def own_kernel(a0, a1, a2lo, a2hi, a3, cturn, own):
    tokens = jnp.concatenate([a0[...], a1[...], a2lo[...], a2hi[...], a3[...]], axis=0)
    own[...] = lax.dot_general(cturn[:HD], tokens, NN, preferred_element_type=F32)


def own_part(pieces, cturn):
    rows, width = pieces[0].shape
    flat = SIDE * rows
    return pl.pallas_call(
        own_kernel,
        grid=(width // TILE,),
        in_specs=[cols_spec(piece.shape[0], TILE) for piece in pieces] + [whole_spec(HD, flat)],
        out_specs=cols_spec(HD, TILE),
        out_shape=jax.ShapeDtypeStruct((HD, width), F32),
        cost_estimate=cost(2 * width * flat * HD, 12 * width * HD),
        name="own_part",
    )(*pieces, cturn)


def grad_kernel(a0, a1, a2lo, a2hi, a3, cturn, up, down, rest):
    j = pl.program_id(0)
    mid = pl.num_programs(0) // 2
    tokens = jnp.concatenate([a0[...], a1[...], a2lo[...], a2hi[...], a3[...]], axis=0)
    grads = lax.dot_general(cturn[HD:], tokens, NN, preferred_element_type=F32)
    ahead = grads[:HD].astype(BF16)
    across = grads[HD : 2 * HD].astype(BF16)
    behind = grads[2 * HD :].astype(BF16)

    @pl.when(j < mid)
    def _():
        up[...] = across
        down[...] = behind
        rest[...] = ahead

    @pl.when(j >= mid)
    def _():
        up[...] = ahead
        down[...] = across
        rest[...] = behind


def grad_parts(pieces, cturn):
    rows, width = pieces[0].shape
    flat = SIDE * rows
    mid = width // TILE // 2
    stacked = pl.BlockSpec((HD, TILE), lambda j: (j // mid, j % mid))
    return pl.pallas_call(
        grad_kernel,
        grid=(width // TILE,),
        in_specs=[cols_spec(piece.shape[0], TILE) for piece in pieces]
        + [whole_spec(SIDE * HD, flat)],
        out_specs=[stacked] * 3,
        out_shape=[jax.ShapeDtypeStruct((2 * HD, width // 2), BF16)] * 3,
        cost_estimate=cost(2 * width * SIDE * flat * HD, 9 * width * HD * 2),
        name="grad_parts",
    )(*pieces, cturn)


def input_product(mine, theirs, cots):
    first = pl.program_id(0) < pl.num_programs(0) // 2
    weights = jnp.concatenate(
        [jnp.where(first, mine[k], theirs[k]) for k in range(SIDE)], axis=1
    )
    return lax.dot_general(cots, weights, NT, preferred_element_type=F32)


def input_kernel(spots, mine, theirs, cots, out):
    lined = jnp.concatenate([cots[k] for k in range(SIDE)], axis=1)
    out[...] = input_product(mine, theirs, lined).astype(BF16)


def input_parts(spots, gathered, cots):
    piece = gathered[0].shape[1]
    flat = cots.shape[1]
    mid = piece // PART
    place = lambda j, spots: (spots[2] + j // mid) % 2 * mid + j % mid
    return pl.pallas_call(
        input_kernel,
        grid_spec=pltpu.PrefetchScalarGridSpec(
            num_scalar_prefetch=1,
            grid=(2 * mid,),
            in_specs=[
                pl.BlockSpec((SIDE, PART, HD), lambda j, spots: (0, jnp.minimum(j, mid - 1), 0)),
                pl.BlockSpec((SIDE, PART, HD), lambda j, spots: (0, jnp.maximum(j - mid, 0), 0)),
                pl.BlockSpec((SIDE, flat, HD), lambda j, spots: (0, 0, 0)),
            ],
            out_specs=pl.BlockSpec((flat, PART), lambda j, spots: (0, place(j, spots))),
        ),
        out_shape=jax.ShapeDtypeStruct((flat, 2 * piece), BF16),
        cost_estimate=cost(4 * piece * SIDE * flat * HD, 18 * piece * HD * 2),
        compiler_params=pltpu.CompilerParams(vmem_limit_bytes=VMEM),
        name="input_parts",
    )(spots, *gathered, cots)


def merge_kernel(fb, own, pl_lo, pl_hi, su_lo, su_hi, qrows, *refs):
    merged, keep, give = refs[-3:]
    j = pl.program_id(0)
    mid = pl.num_programs(0) // 2
    base = fb[...].astype(F32) + own[...]

    def finish(plain, summed):
        total = base + (plain[...].astype(F32) + summed[...].astype(F32))
        merged[...] = total
        share = dot3(halves(qrows[...]), halves(total), NN)
        keep[...] = share[: RANK // 2]
        give[...] = share[RANK // 2 :].astype(BF16)

    @pl.when(j < mid)
    def _():
        finish(pl_lo, su_lo)

    @pl.when(j >= mid)
    def _():
        finish(pl_hi, su_hi)


def merge(feedback, own, sums, qrows, part, before):
    got_up, got_down, sum_up, sum_down = sums
    width = own.shape[1]
    steps = width // WIDE
    mid = steps // 2
    first = part * steps
    shifted = lambda rows: pl.BlockSpec((rows, WIDE), lambda j: (0, first + j))
    low = pl.BlockSpec((HD, WIDE), lambda j: (0, jnp.minimum(j, mid - 1)))
    high = pl.BlockSpec((HD, WIDE), lambda j: (1, jnp.maximum(j - mid, 0)))
    high_from = pl.BlockSpec((HD, WIDE), lambda j: (0, jnp.maximum(j - mid, 0)))
    return pl.pallas_call(
        merge_kernel,
        grid=(steps,),
        in_specs=[shifted(HD), cols_spec(HD, WIDE), low, high, low, high_from, whole_spec(RANK, HD)]
        + [ANY_SPEC] * len(before),
        out_specs=[shifted(HD), shifted(RANK // 2), shifted(RANK // 2)],
        out_shape=[
            jax.ShapeDtypeStruct((HD, 2 * width), F32),
            jax.ShapeDtypeStruct((RANK // 2, 2 * width), F32),
            jax.ShapeDtypeStruct((RANK // 2, 2 * width), BF16),
        ],
        input_output_aliases={7 + k: k for k in range(len(before))},
        cost_estimate=cost(6 * width * RANK * HD, 14 * width * HD),
        name="merge",
    )(feedback, own, got_down, got_up, sum_up, sum_down, qrows, *before)


def ordered(core, mine, theirs):
    first = jnp.where(core == 0, mine[...], theirs[...])
    second = jnp.where(core == 0, theirs[...], mine[...])
    return jnp.concatenate([first, second], axis=0)


def gram_kernel(spots, mine, theirs, merged, right, gram):
    @pl.when(pl.program_id(0) == 0)
    def _():
        gram[...] = jnp.zeros_like(gram)
        right[...] = jnp.zeros_like(right)

    pt = ordered(spots[2], mine, theirs)
    right[...] += dot2(halves(merged[...]), pt, NT)
    gram[...] += lax.dot_general(pt, pt, NT, preferred_element_type=F32)


def gram_of(spots, mine, theirs, merged):
    width = merged.shape[1]
    half = RANK // 2
    return pl.pallas_call(
        gram_kernel,
        grid=(width // LONG,),
        in_specs=[SMEM_SPEC, cols_spec(half, LONG), cols_spec(half, LONG), cols_spec(HD, LONG)],
        out_specs=[whole_spec(HD, RANK), whole_spec(RANK, RANK)],
        out_shape=[
            jax.ShapeDtypeStruct((HD, RANK), F32),
            jax.ShapeDtypeStruct((RANK, RANK), F32),
        ],
        cost_estimate=cost(6 * width * RANK * (RANK + HD), 6 * width * HD),
        compiler_params=pltpu.CompilerParams(vmem_limit_bytes=VMEM),
        name="gram",
    )(spots, mine, theirs, merged)


def inverse_kernel(gram, out):
    row = lax.broadcasted_iota(jnp.int32, (RANK, RANK), 0)
    col = lax.broadcasted_iota(jnp.int32, (RANK, RANK), 1)
    eye = jnp.where(row == col, 1.0, 0.0).astype(F32)
    mat = jnp.concatenate([gram[...], eye], axis=1)
    below = lax.broadcasted_iota(jnp.int32, (RANK, 1), 0)
    for k in range(RANK - 1):
        pivot = mat[k : k + 1, :]
        column = mat[:, k : k + 1]
        factor = jnp.where(below > k, column / mat[k : k + 1, k : k + 1], 0.0)
        mat = mat - factor * pivot
    diag = jnp.sum(jnp.where(row == col, mat[:, :RANK], 0.0), axis=1, keepdims=True)
    out[...] = mat[:, RANK:] / jnp.sqrt(diag)


def inverse_factor(gram):
    return pl.pallas_call(
        inverse_kernel,
        out_shape=jax.ShapeDtypeStruct((RANK, RANK), F32),
        cost_estimate=cost(RANK * RANK * RANK * 400, RANK * RANK * 16),
        name="inverse_factor",
    )(gram)


def final_kernel(replicas, spots, inv, rsum, mine, theirs, merged, qt, update, newfb, zhi, zlo):
    @pl.when(pl.program_id(0) == 0)
    def _():
        right = lax.dot_general(inv[...], rsum[...], NT, precision=HI, preferred_element_type=F32)
        right = right * (1.0 / replicas)
        qt[...] = right
        zturn = lax.dot_general(right, inv[...], TN, precision=HI, preferred_element_type=F32)
        zhi[...], zlo[...] = halves(zturn)

    pt = ordered(spots[2], mine, theirs)
    approx = dot2((zhi[...], zlo[...]), pt, NN)
    update[...] = approx.astype(BF16).T
    newfb[...] = (merged[...] - approx).astype(BF16).T


def final(spots, inv, rsum, mine, theirs, merged, replicas):
    width = merged.shape[1]
    half = RANK // 2
    return pl.pallas_call(
        lambda *refs: final_kernel(replicas, *refs),
        grid=(width // WIDE,),
        in_specs=[
            SMEM_SPEC,
            whole_spec(RANK, RANK),
            whole_spec(HD, RANK),
            cols_spec(half, WIDE),
            cols_spec(half, WIDE),
            cols_spec(HD, WIDE),
        ],
        out_specs=[whole_spec(RANK, HD), rows_spec(WIDE, HD), rows_spec(WIDE, HD)],
        out_shape=[
            jax.ShapeDtypeStruct((RANK, HD), F32),
            jax.ShapeDtypeStruct((width, HD), BF16),
            jax.ShapeDtypeStruct((width, HD), BF16),
        ],
        scratch_shapes=[pltpu.VMEM((HD, RANK), BF16)] * 2,
        cost_estimate=cost(6 * width * RANK * HD, 12 * width * HD),
        name="final",
    )(spots, inv, rsum, mine, theirs, merged)


def tied(arrays, others):
    return lax.optimization_barrier((arrays, others))[0]


def neighbours(block, step):
    return step(block, 1), step(block, -1)


def to_pass_on(before, after):
    rows = before.shape[0]
    return before[: rows // 2], after[rows // 2 :]


def gather_line(block, before, after, passed, step):
    return block, after, step(passed[0], 1), step(passed[1], -1), before


def scatter_near(up, down, step):
    return step(up, 1), step(down, -1)


def scatter_far(got_up, got_down, rest, step):
    mid = rest.shape[0] // 2
    low = lambda array: array[:mid].astype(F32)
    high = lambda array: array[mid:].astype(F32)
    sum_up = step((low(rest) + low(got_up)).astype(BF16), 1)
    sum_down = step((high(rest) + high(got_down)).astype(BF16), -1)
    return got_up, got_down, sum_up, sum_down


def sum_left(keep, give):
    chip = (keep + other_core(give).astype(F32)).astype(BF16)
    mid = chip.shape[0] // 2
    near = lambda array: along_dp(array, lambda x, c: (x ^ 1, c))
    far = lambda array: along_dp(array, lambda x, c: (3 - x, c))
    add = lambda a, b: a.astype(F32) + b.astype(F32)
    first, second = chip[:mid], chip[mid:]
    first_pair = add(first, near(first)).astype(BF16)
    second_pair = add(second, far(second)).astype(BF16)
    mine = jnp.concatenate(
        [add(first_pair, far(first_pair)), add(second_pair, near(second_pair))], axis=0
    ).astype(BF16)
    return mine, other_core(mine)


def sum_right(part):
    chip = part + other_core(part)
    ahead = along_dp(chip, lambda x, c: (x + 1, c))
    behind = along_dp(chip, lambda x, c: (x - 1, c))
    across = along_dp(chip, lambda x, c: (x + 2, c))
    return (chip + across) + (ahead + behind)


def local(acts, cot_kv, w_kv, feedback, q_init):
    tokens, width = acts.shape
    half = width // 2
    replicas = lax.axis_size("dp")
    place = lax.axis_index("dp")
    core = place % 2
    spot = lax.axis_index("tensor")
    z, y = spot // SIDE, spot % SIDE
    spots = jnp.stack([z, y, core]).astype(jnp.int32)
    in_y = lambda array, k: along_tensor(array, 0, k)
    in_z = lambda array, k: along_tensor(array, k, 0)
    lines_z = [[z * SIDE + y for z in range(SIDE)] for y in range(SIDE)]
    lines_y = [[z * SIDE + y for y in range(SIDE)] for z in range(SIDE)]
    flat = SIDE * tokens

    blocks = acts[:, :half], acts[:, half:]
    near = neighbours(blocks[0], in_y)
    cots = lax.all_to_all(
        cot_kv, "tensor", 0, 0, axis_index_groups=lines_z, tiled=True
    ).reshape(SIDE, flat, HD)
    share = lax.dynamic_slice(w_kv, (core * half, 0), (half, HD))
    weights = lax.all_gather(share, "tensor", axis=0, axis_index_groups=lines_z)

    fb_turned = feedback.T
    qcols = q_init.T
    qrows = jnp.where(
        core == 0, qcols, jnp.concatenate([qcols[RANK // 2 :], qcols[: RANK // 2]], axis=0)
    )
    near, fb_turned, qrows, cots = lax.optimization_barrier((near, fb_turned, qrows, cots))
    cturn = turn_cots(spots, cots)
    pieces = gather_line(blocks[0], *near, to_pass_on(*near), in_y)
    near = neighbours(tied(blocks[1], pieces), in_y)
    up, down, rest_a = grad_parts(pieces, cturn)
    pieces_a = pieces
    got_a = scatter_near(up, down, in_z)
    near, up = lax.optimization_barrier((near, up))
    passed = tied(to_pass_on(*near), got_a)
    pieces = gather_line(blocks[1], *near, passed, in_y)

    weights = tied(weights, (near, got_a))
    shares = input_parts(spots, (weights, other_core(weights)), cots)
    sums_a = scatter_far(*got_a, rest_a, in_z)

    pieces, sums_a, shares = lax.optimization_barrier((pieces, sums_a, shares))
    up, down, rest_b = grad_parts(pieces, cturn)
    later, up = lax.optimization_barrier(((pieces_a, pieces), up))
    own_a, own_b = own_part(later[0], cturn), own_part(later[1], cturn)
    got_b = scatter_near(up, down, in_z)
    input_grad = lax.psum_scatter(
        tied(shares, up), "tensor", scatter_dimension=0, axis_index_groups=lines_y, tiled=True
    )

    got_b, own_a, own_b = lax.optimization_barrier((got_b, own_a, own_b))
    left = merge(fb_turned, own_a, tied(sums_a, got_b), qrows, 0, ())
    sums_b = scatter_far(*got_b, rest_b, in_z)
    sums_b, left = lax.optimization_barrier((sums_b, left))
    merged, keep, give = merge(fb_turned, own_b, sums_b, qrows, 1, left)
    mine, theirs = sum_left(keep, give)
    right, gram = gram_of(spots, mine, theirs, merged)
    inv = inverse_factor(gram)
    rsum = sum_right(right)
    qt, update, new_feedback = final(spots, inv, rsum, mine, theirs, merged, replicas)
    return input_grad, update, qt.T, new_feedback


def solution(mesh):
    placed = (
        P(("dp", "tensor"), None),
        P("dp", "tensor"),
        P(None, "tensor"),
        P("dp", "tensor"),
        P("tensor", None),
    )
    return jax.shard_map(
        local,
        mesh=mesh,
        in_specs=placed,
        out_specs=(
            P(("dp", "tensor"), None),
            P(None, "tensor"),
            P("tensor", None),
            P("dp", "tensor"),
        ),
        check_vma=False,
    )
```
